512 devices in a mesh: dp: 8 (over y_lo, core), tensor: 32 (over z, x), section: 2 (over y_hi).
Axes of the slice: x: 4, y: 8 (y_hi: 2, y_lo: 4; y = y_hi * 4 + y_lo), z: 8, core: 2. Of those that a mesh axis runs over, the one named last changes fastest.
Arguments:
- structure_trunk_gradient: bfloat16 [6144, 10240], P(('dp', 'tensor', 'section')), may hold values from -6 to 6
- context: bfloat16 [6144, 5120], P(('dp', 'section'), 'tensor'), may hold values from -6 to 6
- residual: bfloat16 [6144, 10240], P(('dp', 'section'), 'tensor'), may hold values from -16 to 16
- gain: bfloat16 [10240], P('tensor'), may hold values from 0.5 to 1.5
- codes: bfloat16 [5120, 10240], P(None, 'tensor'), may hold values from -0.15625 to 0.15625
- exponents: int32 [40, 160], P(None, 'tensor'), may hold values from -3 to 1
- adapter_down_factor: bfloat16 [5120, 16], P('tensor'), may hold values from -0.078125 to 0.078125
- adapter_up_factor: bfloat16 [16, 10240], P(None, 'tensor'), may hold values from -1.5 to 1.5
- token_residue_map: int32 [16, 384], P(('dp', 'section')), may hold values from 0 to 383, each once within a row
- lengths: int32 [16], P(('dp', 'section')), may hold values from 192 to 384, as said below
Outputs:
- context_gradient: bfloat16 [5120, 6144], P('tensor', ('dp', 'section'))
- hidden_gradient: bfloat16 [6144, 10240], P(('dp', 'section'), 'tensor')
- down_factor_gradient: float32 [5120, 16], P('tensor')
- up_factor_gradient: float32 [16, 10240], P(None, 'tensor')
- final_hidden: bfloat16 [6144, 10240], P(('dp', 'section'), 'tensor')
The draws below stay inside these ranges and needn't reach their ends.
Inputs may be any that keep to these rules, and one draw needn't show every extreme that they name: `token_residue_map`: each row is a permutation of 0 to 383. `lengths`: one crop has 384 valid tokens and one has 192.
All inputs are finite; a program needn't handle non-finite values.
Results may differ from the reference program's by a relative error of at most 0.015.
Values may be sent and summed in bfloat16 or wider, within the bound.
A program may use at most 64 MiB of HBM per device.

```python
import jax
import jax.numpy as jnp
from jax import lax

MODEL_WIDTH = 10240
OUTPUT_HEAD_DIMS = 5120
ADAPTER_RANK = 16
BLKR = 128
BLKC = 64
CROP = 384
CROPS = 16
TOKENS = 6144
N_TENSOR = 32


def draw_residual(key, part):
    key = jax.random.fold_in(key, 11)
    first_key, second_key = jax.random.split(key)
    columns = jnp.arange(MODEL_WIDTH, dtype=jnp.float32) / MODEL_WIDTH
    column_scale = 0.3 * jnp.power(10.0, columns - 0.5)[None, :]
    base = jnp.clip(jax.random.normal(first_key, (TOKENS, MODEL_WIDTH), jnp.float32), -5.0, 5.0)
    row_scale = jnp.power(10.0, jax.random.uniform(second_key, (TOKENS, 1), jnp.float32, -0.5, 0.5))
    return (base * row_scale * column_scale).astype(jnp.bfloat16)


def draw_lengths(key, part):
    key = jax.random.fold_in(key, 5)
    first_key, second_key = jax.random.split(key)
    drawn = jax.random.randint(first_key, (CROPS,), CROP // 2, CROP + 1, jnp.int32)
    order = jax.random.permutation(second_key, CROPS)
    drawn = drawn.at[order[0]].set(CROP)
    drawn = drawn.at[order[1]].set(CROP // 2)
    return drawn.astype(jnp.int32)


def with_ends(values, rng, least, top_value):
    dims = values.shape
    place = [jax.random.randint(jax.random.fold_in(rng, axis), (), 0, dims[axis]) for axis in range(len(dims))]
    values = values.at[tuple(place)].set(least)
    longest = dims.index(max(dims))
    place[longest] = (place[longest] + 1) % dims[longest]
    return values.at[tuple(place)].set(top_value)


def with_spikes(entries, rng, source, target, shards_of, factor):
    def block_of(dim):
        return (jnp.arange(entries.shape[dim]) // (entries.shape[dim] // shards_of)).reshape((-1,) + (1,) * (entries.ndim - 1 - dim))

    one_side = jax.random.permutation(rng, shards_of)[block_of(target)]
    other_side = (block_of(target) + shards_of // 2) % shards_of
    return jnp.where((block_of(source) == one_side) | (block_of(source) == other_side), factor * entries, entries)


def block_scale(key, extent, shards, least, largest):
    level = 1.0
    for axis_at, parts in shards:
        heights = jax.random.uniform(jax.random.fold_in(jax.random.fold_in(key, 6), axis_at), (parts,), jnp.float32, least / len(shards), largest / len(shards))
        level = level * jnp.repeat(jnp.exp(heights), extent[axis_at] // parts).reshape((-1,) + (1,) * (len(extent) - 1 - axis_at))
    return level


def scatter_about(rng, extent, scale, most, cuts=(), kind=jnp.bfloat16):
    values = jax.random.normal(rng, extent, jnp.float32) * scale
    if len(cuts) > 0:
        values = block_scale(rng, extent, cuts, -0.22, 0.18) * values
    return jnp.clip(values, min=-most, max=most).astype(kind)


def gaussian_with(key, shape, scale, most, cuts, heavy, held_as=jnp.bfloat16):
    result = scale * jax.random.normal(key, shape, jnp.float32)
    if cuts:
        result = result * block_scale(key, shape, cuts, -0.22, 0.18)
    return jnp.clip(with_spikes(result, jax.random.fold_in(key, 3), *heavy), -most, most).astype(held_as)


def setup_inputs(seed: int = 0) -> dict:
    seeds = jax.random.split(jax.random.key(seed), 11)
    return {
        "structure_trunk_gradient": scatter_about(seeds[0], (TOKENS, MODEL_WIDTH), 1.0, 6.0, ((0, 512),)),
        "context": scatter_about(seeds[1], (TOKENS, OUTPUT_HEAD_DIMS), 1.0, 6.0, ((0, 16), (1, 32))),
        "residual": draw_residual(jax.random.fold_in(seeds[10], 71), 0),
        "gain": jnp.clip(1.0 + 0.1 * jax.random.normal(seeds[3], (MODEL_WIDTH,), jnp.float32), 0.5, 1.5).astype(jnp.bfloat16),
        "codes": gaussian_with(seeds[4], (OUTPUT_HEAD_DIMS, MODEL_WIDTH), OUTPUT_HEAD_DIMS ** -0.5, 0.15625, ((1, 32),), (0, 1, 32, 2.75)),
        "exponents": with_ends(jax.random.randint(seeds[5], (OUTPUT_HEAD_DIMS // BLKR, MODEL_WIDTH // BLKC), -3, 2), jax.random.fold_in(seeds[5], 1), -3, 1).astype(jnp.int32),
        "adapter_down_factor": scatter_about(seeds[6], (OUTPUT_HEAD_DIMS, ADAPTER_RANK), OUTPUT_HEAD_DIMS ** -0.5, 0.078125, ((0, 32),)),
        "adapter_up_factor": scatter_about(seeds[7], (ADAPTER_RANK, MODEL_WIDTH), ADAPTER_RANK ** -0.5, 1.5, ((1, 32),)),
        "token_residue_map": jax.vmap(lambda own: jax.random.permutation(own, CROP))(jax.random.split(seeds[8], CROPS)).reshape((CROPS, CROP)).astype(jnp.int32),
        "lengths": draw_lengths(jax.random.fold_in(seeds[10], 71), 0),
    }


ADAPTER_SCALE = 2.0

def dequantize(codes, exponents):
    block_rows = codes.shape[0] // exponents.shape[0]
    block_cols = codes.shape[1] // exponents.shape[1]
    factor = jnp.exp2(exponents.astype(jnp.float32))
    spread = codes.astype(jnp.float32).reshape(exponents.shape[0], block_rows, exponents.shape[1], block_cols)
    return (spread * factor[:, None, :, None]).reshape(codes.shape).astype(jnp.bfloat16)

def pick_rows(crop_rows, crop_map):
    return jnp.take(crop_rows, crop_map, axis=0)

def reference(structure_trunk_gradient, context, residual, gain, codes, exponents, adapter_down_factor, adapter_up_factor, token_residue_map, lengths):
    grouped = structure_trunk_gradient.reshape(CROPS, CROP, MODEL_WIDTH)
    picked = jax.vmap(pick_rows)(grouped, token_residue_map)
    positions = jnp.arange(CROP, dtype=jnp.int32)[None, :]
    valid = positions < lengths[:, None]
    upstream = jnp.where(valid[:, :, None], picked.astype(jnp.float32), 0.0).reshape(TOKENS, MODEL_WIDTH)
    weights = dequantize(codes, exponents)
    inner_product = jnp.dot(context, adapter_down_factor, preferred_element_type=jnp.float32).astype(jnp.bfloat16)
    hidden_state = jnp.dot(context, weights, preferred_element_type=jnp.float32)
    hidden_state = hidden_state + ADAPTER_SCALE * jnp.dot(inner_product, adapter_up_factor, preferred_element_type=jnp.float32)
    hidden_state = hidden_state + residual.astype(jnp.float32)
    average = lax.optimization_barrier(jnp.sum(hidden_state, axis=1)) / MODEL_WIDTH
    variance = lax.optimization_barrier(jnp.sum(hidden_state * hidden_state, axis=1)) / MODEL_WIDTH - average * average
    inverse = lax.rsqrt(variance + 1e-05)
    normed = (hidden_state - average[:, None]) * inverse[:, None]
    final_hidden = (gain.astype(jnp.float32)[None, :] * normed).astype(jnp.bfloat16)
    scaled = gain.astype(jnp.float32)[None, :] * upstream
    first_mean = lax.optimization_barrier(jnp.sum(scaled, axis=1)) / MODEL_WIDTH
    second_mean = lax.optimization_barrier(jnp.sum(scaled * normed, axis=1)) / MODEL_WIDTH
    hidden_gradient = (inverse[:, None] * (scaled - first_mean[:, None] - normed * second_mean[:, None])).astype(jnp.bfloat16)
    contract_product = (((1,), (1,)), ((), ()))
    passed_through = lax.dot_general(hidden_gradient, adapter_up_factor, contract_product, preferred_element_type=jnp.float32).astype(jnp.bfloat16)
    group_cols = MODEL_WIDTH // N_TENSOR

    def add_group(total, group):
        start = (group * group_cols).astype(jnp.int32)
        weight_cols = lax.dynamic_slice_in_dim(weights, start, group_cols, 1)
        grad_cols = lax.dynamic_slice_in_dim(hidden_gradient, start, group_cols, 1)
        partial_term = lax.dot_general(weight_cols, grad_cols, contract_product, preferred_element_type=jnp.float32)
        rounded = lax.optimization_barrier(partial_term.astype(jnp.bfloat16)).astype(jnp.float32)
        return (total + rounded, None)
    partial_total_sum, _ = lax.scan(add_group, jnp.zeros((OUTPUT_HEAD_DIMS, TOKENS), jnp.float32), jnp.arange(N_TENSOR, dtype=jnp.int32))
    adapter_term = lax.dot_general(adapter_down_factor, passed_through, contract_product, preferred_element_type=jnp.float32)
    context_gradient = (partial_total_sum + ADAPTER_SCALE * adapter_term).astype(jnp.bfloat16)
    row_contraction = (((0,), (0,)), ((), ()))
    down_factor_gradient = ADAPTER_SCALE * lax.dot_general(context, passed_through, row_contraction, preferred_element_type=jnp.float32)
    up_factor_gradient = ADAPTER_SCALE * lax.dot_general(inner_product, hidden_gradient, row_contraction, preferred_element_type=jnp.float32)
    return (context_gradient, hidden_gradient, down_factor_gradient, up_factor_gradient, final_hidden)
```

```python
import functools

import jax
import jax.numpy as jnp
from jax import lax
from jax.experimental import pallas as pl
from jax.experimental.pallas import tpu as pltpu
from jax.sharding import PartitionSpec as P

MODEL_WIDTH = 10240
DIMS = 5120
ADAPTER_SCALE = 2.0
CROP = 384
COLS = 320
ROWS = 160
RANK = 16
NX = 4
NZ = 8
NY = 8
BLKR = 128
BLKC = 64
OWNED = 12
SLOT = 16
F32 = jnp.float32
BF16 = jnp.bfloat16
MESH = pl.DeviceIdType.MESH
QR = 96
PR = 80
CR = QR + PR
TOKEN_BLOCK = 128
NBLOCK = CROP // TOKEN_BLOCK

SENDS = 200


def dot(a, b, dims=((1,), (0,))):
    return lax.dot_general(a, b, (dims, ((), ())), preferred_element_type=F32)


def kernel(
    grad_ref, ctx_ref, res_ref, gain_ref, codes_ref, exp_ref, down_ref, up_ref, map_ref, len_ref,
    cg_ref, hg_ref, dg_ref, ug_ref, fh_ref,
    W, C, WT, WX, GM, GR, ACC, RT, HX, PART, RS, RR, LR, UP4, ST, SX, SZ, TH, TZ, GA, GC, GY, GS,
    send_sem, recv_sem, load_sem, gsend_sem, grecv_sem,
):
    dp = lax.axis_index("dp")
    t = lax.axis_index("tensor")
    sec = lax.axis_index("section")
    x = lax.rem(t, NX)
    z = lax.div(t, NX)
    core = lax.rem(dp, 2)
    y = sec * (NY // 2) + lax.div(dp, 2)

    def dev_x(r):
        return (dp, z * NX + lax.rem(x + r, NX), sec)

    def dev_z(r):
        return (dp, lax.rem(z + r, NZ) * NX + x, sec)

    def dev_y(r):
        other = lax.rem(y + r, NY)
        return (lax.rem(other, NY // 2) * 2 + core, t, lax.div(other, NY // 2))

    other_core = (dp + 1 - 2 * core, t, sec)
    target_sec = lax.div(t, 16)
    self_target = (target_sec == sec).astype(jnp.int32)

    def w_rows(index):
        return pl.ds(pl.multiple_of(index * ROWS, 32), ROWS)

    load = pltpu.make_async_copy(codes_ref, W, load_sem)
    load.start()

    barrier = pltpu.get_barrier_semaphore()

    def greet(device):
        pl.semaphore_signal(barrier, inc=1, device_id=device, device_id_type=MESH)

    for r in range(1, NX):
        greet(dev_x(r))
    for r in range(1, NZ):
        greet(dev_z(r))
    for r in range(1, NY):
        greet(dev_y(r))
    greet(other_core)

    @pl.loop(0, 32)
    def _(i):
        src_t = sec * 16 + lax.div(i, 2)
        src_s = lax.rem(i, 2)

        @pl.when(jnp.logical_or(src_t != t, src_s != sec))
        def _():
            greet((dp, src_t, src_s))

    counter = [0]

    def copy(src, dst, device):
        k = counter[0]
        counter[0] += 1
        return pltpu.make_async_remote_copy(
            src_ref=src, dst_ref=dst, send_sem=send_sem.at[k], recv_sem=recv_sem.at[k],
            device_id=device, device_id_type=MESH,
        )

    pending = []

    def start(c):
        c.start()
        pending.append(c)
        return c

    C[0, 0:ROWS, :] = ctx_ref[...].astype(F32).T.astype(BF16)
    C[0, ROWS:CR, :] = jnp.zeros((RANK, CROP), BF16)
    C[0, ROWS:CR, 0:ROWS] = down_ref[...].astype(F32).T.astype(BF16)
    UP4[0] = up_ref[...]
    GM[...] = jnp.zeros_like(GM)
    for i in range(32):
        GM[i, 0:OWNED, :] = grad_ref[:, i * COLS : (i + 1) * COLS]

    pl.semaphore_wait(barrier, (NX - 1) + (NZ - 1) + (NY - 1) + 1 + 32 - self_target)

    def q_rows(slot):
        return C.at[slot, 0:QR]

    def p_rows(rz):
        return C.at[pl.ds(rz * NX, NX), QR:CR]

    def z_ring_q(step):
        if step < 4:
            right = copy(q_rows(((NZ - step + 1) % NZ) * NX), q_rows((NZ - step) * NX), dev_z(1))
            left = copy(q_rows((step - 1) * NX), q_rows(step * NX), dev_z(NZ - 1))
        else:
            right = copy(C.at[5 * NX, 0:48], C.at[4 * NX, 0:48], dev_z(1))
            left = copy(C.at[3 * NX, 48:QR], C.at[4 * NX, 48:QR], dev_z(NZ - 1))
        return start(right), start(left)

    def z_ring_p(step):
        if step < 4:
            right = copy(p_rows((NZ - step + 1) % NZ), p_rows(NZ - step), dev_z(1))
            left = copy(p_rows(step - 1), p_rows(step), dev_z(NZ - 1))
        else:
            right = copy(C.at[5 * NX : 6 * NX, QR : QR + 48], C.at[4 * NX : 5 * NX, QR : QR + 48], dev_z(1))
            left = copy(C.at[3 * NX : 4 * NX, QR + 48 : CR], C.at[4 * NX : 5 * NX, QR + 48 : CR], dev_z(NZ - 1))
        return start(right), start(left)

    def x_first(rz, lo, hi):
        b = rz * NX
        right = copy(C.at[b, lo:hi], C.at[b + 3, lo:hi], dev_x(1))
        left = copy(C.at[b, lo:hi], C.at[b + 1, lo:hi], dev_x(NX - 1))
        return start(right), start(left)

    def x_second(rz, lo, mid, hi):
        b = rz * NX
        right = copy(C.at[b + 3, lo:mid], C.at[b + 2, lo:mid], dev_x(1))
        left = copy(C.at[b + 1, mid:hi], C.at[b + 2, mid:hi], dev_x(NX - 1))
        return start(right), start(left)

    def arrived(pair):
        for c in pair:
            c.wait_recv()

    qz1 = z_ring_q(1)
    px1 = x_first(0, QR, CR)
    qx1 = {0: x_first(0, 0, QR)}
    qx2 = {}
    upc = [start(copy(UP4.at[0], UP4.at[NX - r], dev_x(r))) for r in range(1, NX)]

    my_slot = lax.rem(t, 16) * 2 + sec

    def grad_copy(to):
        return pltpu.make_async_remote_copy(
            src_ref=GM.at[to], dst_ref=GR.at[my_slot], send_sem=gsend_sem, recv_sem=grecv_sem,
            device_id=(dp, to, target_sec), device_id_type=MESH,
        )

    local = pltpu.make_async_copy(GM.at[t], GR.at[my_slot], grecv_sem)

    @pl.when(self_target == 1)
    def _():
        local.start()

    @pl.when(self_target == 0)
    def _():
        grad_copy(t).start()

    @pl.loop(1, 32)
    def _(i):
        grad_copy(lax.rem(t + i, 32)).start()

    load.wait()
    codes_scale = exp_ref[...]
    factor = jnp.where(
        codes_scale == -3, 0.125,
        jnp.where(codes_scale == -2, 0.25, jnp.where(codes_scale == -1, 0.5, jnp.where(codes_scale == 0, 1.0, 2.0))),
    ).astype(F32)
    lane = lax.broadcasted_iota(jnp.int32, (DIMS // BLKR, COLS), 1)
    spread = jnp.zeros((DIMS // BLKR, COLS), F32)
    for j in range(COLS // BLKC):
        spread = jnp.where(lax.div(lane, BLKC) == j, factor[:, j : j + 1], spread)
    GS[...] = spread

    arrived(px1)
    px2 = x_second(0, QR, QR + 48, CR)
    arrived(qz1)
    qz2 = z_ring_q(2)
    for rz in (1, 7):
        qx1[rz] = x_first(rz, 0, QR)

    @pl.loop(0, DIMS // BLKR)
    def _(b):
        rows = pl.ds(pl.multiple_of(b * BLKR, BLKR), BLKR)
        W[rows, :] = (W[rows, :].astype(F32) * GS[pl.ds(b, 1), :]).astype(BF16)

    wx = []
    for r in range(1, NX):
        block = y * NX + lax.rem(x + r, NX)
        rows = pl.ds(pl.multiple_of(block * ROWS + core * (ROWS // 2), 16), ROWS // 2)
        wx.append(start(copy(W.at[rows], WX.at[NX - r, y, core], dev_x(r))))

    arrived(px2)
    pz1 = z_ring_p(1)
    arrived(qx1[0])
    qx2[0] = x_second(0, 0, 48, QR)
    arrived(qz2)
    qz3 = z_ring_q(3)
    for rz in (2, 6):
        qx1[rz] = x_first(rz, 0, QR)

    def turn(lo, hi):
        @pl.loop(lo, hi)
        def _(b):
            WT[b, 0:COLS, :] = W[w_rows(b), :].astype(F32).T.astype(BF16)

    def y_unit(rel):
        return WX.at[1:NX, lax.rem(y + rel, NY), core]

    def y_ring(step):
        if step < 4:
            a = y_unit(NY - step + 1)
            right = copy(a, a, dev_y(1))
            b = y_unit(step - 1)
            left = copy(b, b, dev_y(NY - 1))
        else:
            a = WX.at[1:NX, lax.rem(y + 5, NY), core, 0:48]
            right = copy(a, a, dev_y(1))
            b = WX.at[1:NX, lax.rem(y + 3, NY), core, 48:80]
            left = copy(b, b, dev_y(NY - 1))
        return start(right), start(left)

    swaps = []

    def core_swap(rel):
        a = y_unit(rel)
        swaps.append(start(copy(a, a, other_core)))

    turn(0, 8)
    for c in wx:
        c.wait_recv()
    y1 = y_ring(1)
    core_swap(0)
    arrived(qz3)
    qz4 = z_ring_q(4)
    for rz in (3, 5):
        qx1[rz] = x_first(rz, 0, QR)
    for rz in (1, 7):
        arrived(qx1[rz])
        qx2[rz] = x_second(rz, 0, 48, QR)
    arrived(pz1)
    pz2 = z_ring_p(2)
    turn(8, 16)
    arrived(qz4)
    qx1[4] = x_first(4, 0, QR)
    for rz in (2, 6):
        arrived(qx1[rz])
        qx2[rz] = x_second(rz, 0, 48, QR)
    arrived(y1)
    y2 = y_ring(2)
    core_swap(1)
    core_swap(7)
    turn(16, 32)

    ACC[...] = jnp.zeros_like(ACC)

    def forward(rz):
        @pl.loop(0, NX)
        def _(rx):
            source = lax.rem(z + rz, NZ) * NX + lax.rem(x + rx, NX)
            slot = rz * NX + rx
            WT[source, COLS : COLS + RANK, :] = C[slot, ROWS:CR, 0:ROWS]
            ACC[...] += dot(WT[source], C[slot, 0:ROWS, :])

    arrived(qx2[0])
    forward(0)
    arrived(pz2)
    pz3 = z_ring_p(3)
    for rz in (3, 5):
        arrived(qx1[rz])
        qx2[rz] = x_second(rz, 0, 48, QR)
    arrived(y2)
    y3 = y_ring(3)
    core_swap(2)
    core_swap(6)
    for rz in (1, 7):
        arrived(qx2[rz])
        forward(rz)

    RT[...] = res_ref[...].astype(F32).T
    WX[0] = jnp.stack([W[w_rows(k * NX + x), :] for k in range(NZ)]).reshape(NZ, 2, ROWS // 2, COLS)
    grad_all = pltpu.make_async_copy(GR, GR, grecv_sem)
    grad_all.wait()
    residue = map_ref[...]
    block = lax.shift_right_logical(residue * 43691, 19)
    place = block * SLOT + (residue - block * OWNED)
    token = lax.broadcasted_iota(jnp.int32, (1, CROP), 1)
    place = jnp.where(token < len_ref[0], place, -1)
    chosen = (lax.broadcasted_iota(jnp.int32, (32 * SLOT, CROP), 0) == place).astype(F32).astype(BF16)
    upstream = dot(GR[...].reshape(32 * SLOT, COLS), chosen, ((0,), (0,)))
    gain = jnp.broadcast_to(gain_ref[...].astype(F32), (8, COLS)).T[:, 0:1]
    scaled = gain * upstream

    arrived(pz3)
    pz4 = z_ring_p(4)
    arrived(qx1[4])
    qx2[4] = x_second(4, 0, 48, QR)
    arrived(y3)
    y4 = y_ring(4)
    core_swap(3)
    core_swap(5)
    for rz in (2, 6):
        arrived(qx2[rz])
        forward(rz)
    for rz in (3, 5):
        arrived(qx2[rz])
        forward(rz)
    arrived(pz4)
    arrived(qx2[4])
    forward(4)

    inner = ACC[COLS : COLS + RANK, :].astype(BF16)
    hidden = ACC[0:COLS, :] + ADAPTER_SCALE * dot(up_ref[...], inner, ((0,), (0,))) + RT[...]
    ST[0:1, :] = jnp.sum(hidden, axis=0, keepdims=True)
    ST[1:2, :] = jnp.sum(hidden * hidden, axis=0, keepdims=True)
    ST[2:3, :] = jnp.sum(scaled, axis=0, keepdims=True)
    ST[3:4, :] = jnp.sum(scaled * hidden, axis=0, keepdims=True)
    ST[4:8, :] = jnp.zeros((4, CROP), F32)
    sx = [start(copy(ST, SX.at[r], dev_x(r))) for r in range(1, NX)]
    for c in sx:
        c.wait_recv()
    SZ[0] = (ST[...] + SX[1]) + (SX[2] + SX[3])
    sz = [start(copy(SZ.at[0], SZ.at[r], dev_z(r))) for r in range(1, NZ)]
    arrived(y4)
    core_swap(4)
    for c in sz:
        c.wait_recv()
    sums = jnp.sum(SZ[...], axis=0) / MODEL_WIDTH
    average = sums[0:1, :]
    variance = sums[1:2, :] - average * average
    inverse = lax.rsqrt(variance + 1e-05)
    first_mean = sums[2:3, :]
    second_mean = inverse * (sums[3:4, :] - average * first_mean)
    normed = (hidden - average) * inverse
    gradient = (inverse * (scaled - first_mean - normed * second_mean)).astype(BF16)
    for b in range(NBLOCK):
        HX[b, 0] = gradient[:, b * TOKEN_BLOCK : (b + 1) * TOKEN_BLOCK]

    def hx_first(b):
        return (
            start(copy(HX.at[b, 0], HX.at[b, 3], dev_x(1))),
            start(copy(HX.at[b, 0], HX.at[b, 1], dev_x(NX - 1))),
        )

    def hx_second(b):
        return (
            start(copy(HX.at[b, 3, 0:160], HX.at[b, 2, 0:160], dev_x(1))),
            start(copy(HX.at[b, 1, 160:COLS], HX.at[b, 2, 160:COLS], dev_x(NX - 1))),
        )

    h1 = [hx_first(b) for b in range(NBLOCK)]

    fh_ref[...] = (gain * normed).T.astype(BF16)
    hidden_gradient = gradient.astype(F32).T.astype(BF16)
    hg_ref[...] = hidden_gradient
    GA[:, 0:COLS] = ADAPTER_SCALE * dot(inner, hidden_gradient)
    for c in upc:
        c.wait_recv()
    for c in swaps:
        c.wait_recv()
    h2 = []
    for b in range(NBLOCK):
        arrived(h1[b])
        h2.append(hx_second(b))

    halves = NZ * ROWS // 2

    def partials(b):
        @pl.loop(0, 2)
        def _(h):
            total = jnp.zeros((halves, TOKEN_BLOCK), F32)
            for r in range(NX):
                w = WX[r, pl.ds(h * (NZ // 2), NZ // 2)].reshape(halves, COLS)
                total = total + dot(w, HX[b, r])
            PART[b, pl.ds(h * (NZ // 2), NZ // 2)] = total.reshape(NZ // 2, ROWS, TOKEN_BLOCK)

    def part(b, rel):
        return PART[b, lax.rem(z + rel, NZ)]

    HALF = ROWS // 2

    def rs_step(b, step):
        if step == 1:
            RS[b, 0, 0, 0:HALF] = part(b, 4)[0:HALF].astype(BF16)
            RS[b, 1, 0, 0:HALF] = part(b, 4)[HALF:ROWS].astype(BF16)
            right = copy(RS.at[b, 0, 0, 0:HALF], RR.at[b, 0, 0:HALF], dev_z(1))
            left = copy(RS.at[b, 1, 0, 0:HALF], LR.at[b, 0, 0:HALF], dev_z(NZ - 1))
        else:
            mine_right, mine_left = part(b, 5 - step), part(b, 3 + step)
            if step == 2:
                RS[b, 0, 1, 0:HALF] = (mine_right[0:HALF] + RR[b, 0, 0:HALF].astype(F32)).astype(BF16)
                RS[b, 0, 1, HALF:ROWS] = mine_right[HALF:ROWS].astype(BF16)
                RS[b, 1, 1, 0:HALF] = mine_left[0:HALF].astype(BF16)
                RS[b, 1, 1, HALF:ROWS] = (mine_left[HALF:ROWS] + LR[b, 0, 0:HALF].astype(F32)).astype(BF16)
            else:
                RS[b, 0, step - 1] = (mine_right + RR[b, step - 2].astype(F32)).astype(BF16)
                RS[b, 1, step - 1] = (mine_left + LR[b, step - 2].astype(F32)).astype(BF16)
            right = copy(RS.at[b, 0, step - 1], RR.at[b, step - 1], dev_z(1))
            left = copy(RS.at[b, 1, step - 1], LR.at[b, step - 1], dev_z(NZ - 1))
        return start(right), start(left)

    rs = {}
    for b in range(NBLOCK):
        arrived(h2[b])
        lanes = slice(b * TOKEN_BLOCK, (b + 1) * TOKEN_BLOCK)
        TZ[0, :, lanes] = jnp.zeros((RANK, TOKEN_BLOCK), F32)

        @pl.loop(0, NX)
        def _(r):
            TZ[0, :, lanes] += dot(UP4[r], HX[b, r])

        if b == NBLOCK - 1:
            tz = [start(copy(TZ.at[0], TZ.at[r], dev_z(r))) for r in range(1, NZ)]
        partials(b)
        rs[b, 1] = rs_step(b, 1)
        if b >= 1:
            arrived(rs[b - 1, 1])
            rs[b - 1, 2] = rs_step(b - 1, 2)
        if b >= 2:
            arrived(rs[b - 2, 2])
            rs[b - 2, 3] = rs_step(b - 2, 3)

    for c in tz:
        c.wait_recv()
    through_all = jnp.sum(TZ[...], axis=0).astype(BF16)
    GA[:, 384 : 384 + ROWS] = ADAPTER_SCALE * dot(through_all, ctx_ref[...])
    GA[:, 384 + ROWS :] = jnp.zeros((RANK, 96), F32)
    GA[:, COLS:384] = jnp.zeros((RANK, 64), F32)
    gc = start(copy(GA, GC, other_core))

    arrived(rs[2, 1])
    rs[2, 2] = rs_step(2, 2)
    arrived(rs[1, 2])
    rs[1, 3] = rs_step(1, 3)
    arrived(rs[0, 3])
    rs[0, 4] = rs_step(0, 4)
    gc.wait_recv()
    GY[0] = GA[...] + GC[...]
    gy = [start(copy(GY.at[0], GY.at[r], dev_y(r))) for r in range(1, NY)]
    arrived(rs[2, 2])
    rs[2, 3] = rs_step(2, 3)
    arrived(rs[1, 3])
    rs[1, 4] = rs_step(1, 4)
    arrived(rs[2, 3])
    rs[2, 4] = rs_step(2, 4)

    adapter = ADAPTER_SCALE * dot(down_ref[...], through_all)
    for b in range(NBLOCK):
        arrived(rs[b, 4])
        lanes = slice(b * TOKEN_BLOCK, (b + 1) * TOKEN_BLOCK)
        total = part(b, 0) + RR[b, 3].astype(F32) + LR[b, 3].astype(F32)
        cg_ref[:, lanes] = (total + adapter[:, lanes]).astype(BF16)

    for c in gy:
        c.wait_recv()
    grads = jnp.sum(GY[...], axis=0)
    ug_ref[...] = grads[:, 0:COLS]
    dg_ref[...] = grads[:, 384 : 384 + ROWS].T

    for c in pending:
        c.wait_send()

    @pl.when(self_target == 1)
    def _():
        pltpu.make_async_copy(GM.at[0:31], GM.at[0:31], gsend_sem).wait()

    @pl.when(self_target == 0)
    def _():
        pltpu.make_async_copy(GM, GM, gsend_sem).wait()


def on_device(grad, context, residual, gain, codes, exponents, down, up, residue_map, lengths):
    vmem = pl.BlockSpec(memory_space=pltpu.VMEM)
    return pl.pallas_call(
        kernel,
        out_shape=(
            jax.ShapeDtypeStruct((ROWS, CROP), BF16),
            jax.ShapeDtypeStruct((CROP, COLS), BF16),
            jax.ShapeDtypeStruct((ROWS, RANK), F32),
            jax.ShapeDtypeStruct((RANK, COLS), F32),
            jax.ShapeDtypeStruct((CROP, COLS), BF16),
        ),
        in_specs=[vmem] * 4
        + [pl.BlockSpec(memory_space=pl.ANY)]
        + [vmem] * 4
        + [pl.BlockSpec(memory_space=pltpu.SMEM)],
        out_specs=[vmem] * 5,
        scratch_shapes=[
            pltpu.VMEM((DIMS, COLS), BF16),
            pltpu.VMEM((NX * NZ, CR, CROP), BF16),
            pltpu.VMEM((NX * NZ, COLS + RANK, ROWS), BF16),
            pltpu.VMEM((NX, NZ, 2, ROWS // 2, COLS), BF16),
            pltpu.VMEM((32, SLOT, COLS), BF16),
            pltpu.VMEM((32, SLOT, COLS), BF16),
            pltpu.VMEM((COLS + RANK, CROP), F32),
            pltpu.VMEM((COLS, CROP), F32),
            pltpu.VMEM((NBLOCK, NX, COLS, TOKEN_BLOCK), BF16),
            pltpu.VMEM((NBLOCK, NZ, ROWS, TOKEN_BLOCK), F32),
            pltpu.VMEM((NBLOCK, 2, 4, ROWS, TOKEN_BLOCK), BF16),
            pltpu.VMEM((NBLOCK, 4, ROWS, TOKEN_BLOCK), BF16),
            pltpu.VMEM((NBLOCK, 4, ROWS, TOKEN_BLOCK), BF16),
            pltpu.VMEM((NX, RANK, COLS), BF16),
            pltpu.VMEM((8, CROP), F32),
            pltpu.VMEM((NX, 8, CROP), F32),
            pltpu.VMEM((NZ, 8, CROP), F32),
            pltpu.VMEM((8, 128), F32),
            pltpu.VMEM((NZ, RANK, CROP), F32),
            pltpu.VMEM((RANK, 640), F32),
            pltpu.VMEM((RANK, 640), F32),
            pltpu.VMEM((NY, RANK, 640), F32),
            pltpu.VMEM((DIMS // BLKR, COLS), F32),
            pltpu.SemaphoreType.DMA((SENDS,)),
            pltpu.SemaphoreType.DMA((SENDS,)),
            pltpu.SemaphoreType.DMA,
            pltpu.SemaphoreType.DMA,
            pltpu.SemaphoreType.DMA,
        ],
        compiler_params=pltpu.CompilerParams(
            collective_id=0, has_side_effects=True, vmem_limit_bytes=56 * 1024 * 1024
        ),
        cost_estimate=pl.CostEstimate(flops=2 * 2 * CROP * DIMS * COLS, bytes_accessed=8 << 20, transcendentals=0),
    )(grad, context, residual, gain.reshape(1, COLS), codes, exponents, down, up, residue_map, lengths)


def solution(mesh):
    in_specs = (
        P(("dp", "tensor", "section"), None),
        P(("dp", "section"), "tensor"),
        P(("dp", "section"), "tensor"),
        P("tensor"),
        P(None, "tensor"),
        P(None, "tensor"),
        P("tensor", None),
        P(None, "tensor"),
        P(("dp", "section"), None),
        P(("dp", "section")),
    )
    out_specs = (
        P("tensor", ("dp", "section")),
        P(("dp", "section"), "tensor"),
        P("tensor", None),
        P(None, "tensor"),
        P(("dp", "section"), "tensor"),
    )
    return jax.shard_map(
        on_device, mesh=mesh, in_specs=in_specs, out_specs=out_specs, check_vma=False
    )
```

```python
import functools

import jax
import jax.numpy as jnp
from jax import lax
from jax.experimental import pallas as pl
from jax.experimental.pallas import tpu as pltpu
from jax.sharding import PartitionSpec as P

MODEL_WIDTH = 10240
DIMS = 5120
ADAPTER_SCALE = 2.0
CROP = 384
COLS = 320
ROWS = 160
RANK = 16
NX = 4
NZ = 8
NY = 8
BLKR = 128
BLKC = 64
OWNED = 12
SLOT = 16
F32 = jnp.float32
BF16 = jnp.bfloat16
MESH = pl.DeviceIdType.MESH
QR = 112
PH = 32
TOKEN_BLOCK = 128
NBLOCK = CROP // TOKEN_BLOCK

SENDS = 200


def dot(a, b, dims=((1,), (0,))):
    return lax.dot_general(a, b, (dims, ((), ())), preferred_element_type=F32)


def kernel(
    grad_hbm, ctx_hbm, res_hbm, gain_ref, codes_hbm, exp_hbm, down_hbm, up_hbm, map_hbm, len_ref,
    cg_out, hg_out, dg_out, ug_out, fh_out,
    W, C, DX, DN, SLAB, WS, WT, WX, GI, GM, A1, A2, A3, ACC, HX, PART, RS, RR, LR, ST, SX, SZ, TX, TZ,
    UA, UC, UY, DA, DC, DY, GS, RES, EXP, DIN, UP, MAP, CG, HG, DG, UG, FH,
    send_sem, recv_sem, load_sem,
):
    dp = lax.axis_index("dp")
    t = lax.axis_index("tensor")
    sec = lax.axis_index("section")
    x = lax.rem(t, NX)
    z = lax.div(t, NX)
    core = lax.rem(dp, 2)
    y = sec * (NY // 2) + lax.div(dp, 2)

    def dev_x(r):
        return (dp, z * NX + lax.rem(x + r, NX), sec)

    def dev_z(r):
        return (dp, lax.rem(z + r, NZ) * NX + x, sec)

    def dev_y(r):
        other = lax.rem(y + r, NY)
        return (lax.rem(other, NY // 2) * 2 + core, t, lax.div(other, NY // 2))

    other_core = (dp + 1 - 2 * core, t, sec)
    before, after, opposite = lax.rem(x + 3, NX), lax.rem(x + 1, NX), lax.rem(x + 2, NX)

    group = NX * ROWS

    def w_lanes(index):
        return pl.ds(pl.multiple_of(index * group, 128), group)

    local_copies = [0]

    def local_copy(src, dst):
        k = local_copies[0]
        local_copies[0] += 1
        c = pltpu.make_async_copy(src, dst, load_sem.at[k])
        c.start()
        return c

    load_ctx = local_copy(ctx_hbm, C.at[x])
    load_grad = local_copy(grad_hbm, GI)
    load_down = local_copy(down_hbm, DIN)
    load_exp = local_copy(exp_hbm, EXP)
    load_codes = local_copy(codes_hbm, W.at[0:COLS])
    load_rest = [local_copy(map_hbm, MAP), local_copy(up_hbm, UP), local_copy(res_hbm, RES)]

    barrier = pltpu.get_barrier_semaphore()

    def greet(device):
        pl.semaphore_signal(barrier, inc=1, device_id=device, device_id_type=MESH)

    for r in range(1, NX):
        greet(dev_x(r))
    for r in range(1, NZ):
        greet(dev_z(r))
    for r in range(1, NY):
        greet(dev_y(r))
    greet(other_core)

    counter = [0]

    def copy(src, dst, device):
        k = counter[0]
        counter[0] += 1
        return pltpu.make_async_remote_copy(
            src_ref=src, dst_ref=dst, send_sem=send_sem.at[k], recv_sem=recv_sem.at[k],
            device_id=device, device_id_type=MESH,
        )

    pending = []

    def start(c):
        c.start()
        pending.append(c)
        return c

    def arrived(pair):
        for c in pair:
            c.wait_recv()

    load_down.wait()
    DX[x] = jnp.concatenate([DIN[...], jnp.zeros((RANK, 96), BF16)], axis=1)
    load_ctx.wait()

    pl.semaphore_wait(barrier, (NX - 1) + (NZ - 1) + (NY - 1) + 1)

    def z_ring(step, column, lo, mid, hi):
        if step < 4:
            right = copy(
                C.at[((NZ - step + 1) % NZ) * NX + column, lo:hi], C.at[(NZ - step) * NX + column, lo:hi], dev_z(1)
            )
            left = copy(C.at[(step - 1) * NX + column, lo:hi], C.at[step * NX + column, lo:hi], dev_z(NZ - 1))
        else:
            right = copy(C.at[5 * NX + column, lo:mid], C.at[4 * NX + column, lo:mid], dev_z(1))
            left = copy(C.at[3 * NX + column, mid:hi], C.at[4 * NX + column, mid:hi], dev_z(NZ - 1))
        return start(right), start(left)

    def qz(step):
        return z_ring(step, x, 0, 64, QR)

    def pz(step, column):
        return z_ring(step, column, QR, QR + PH, ROWS)

    def x_first(rz, lo, hi):
        own = C.at[rz * NX + x, lo:hi]
        return start(copy(own, own, dev_x(1))), start(copy(own, own, dev_x(NX - 1)))

    def x_second(rz, lo, mid, hi):
        a = C.at[rz * NX + before, lo:mid]
        b = C.at[rz * NX + after, mid:hi]
        return start(copy(a, a, dev_x(1))), start(copy(b, b, dev_x(NX - 1)))

    qz_c, qx1, qx2, pz_c = {}, {}, {}, {}

    def q_first(*places):
        for rz in places:
            qx1[rz] = x_first(rz, 0, QR)

    def q_second(*places):
        for rz in places:
            arrived(qx1[rz])
            qx2[rz] = x_second(rz, 0, 64 if rz % 2 == 0 else 48, QR)

    def p_next(step, column, name):
        if step > 1:
            arrived(pz_c[name, step - 1])
        pz_c[name, step] = pz(step, column)

    def dn_ring(step):
        if step < 4:
            right = copy(DN.at[(NZ - step + 1) % NZ], DN.at[NZ - step], dev_z(1))
            left = copy(DN.at[step - 1], DN.at[step], dev_z(NZ - 1))
            return start(right), start(left)
        return (start(copy(DN.at[5], DN.at[4], dev_z(1))),)

    qz_c[1] = qz(1)
    px1 = x_first(0, QR, ROWS)
    dx = [start(copy(DX.at[x], DX.at[x], dev_x(r))) for r in range(1, NX)]
    p_next(1, x, "own")
    q_first(0)

    load_exp.wait()
    codes_scale = EXP[...]
    factor = jnp.where(
        codes_scale == -3, 0.125,
        jnp.where(codes_scale == -2, 0.25, jnp.where(codes_scale == -1, 0.5, jnp.where(codes_scale == 0, 1.0, 2.0))),
    ).astype(F32)
    for j in range(COLS // BLKC):
        GS[j * BLKC : (j + 1) * BLKC, :] = jnp.broadcast_to(factor[j : j + 1, :], (BLKC, DIMS // BLKR))
    load_codes.wait()

    picked = (
        lax.broadcasted_iota(jnp.int32, (DIMS // BLKR, 128), 0)
        == y * (group // BLKR) + lax.broadcasted_iota(jnp.int32, (DIMS // BLKR, 128), 1)
    )
    slab_scale = dot(GS[...].astype(BF16), picked.astype(F32).astype(BF16))
    for i in range(group // BLKR):
        lanes = pl.ds(pl.multiple_of(y * group + i * BLKR, BLKR), BLKR)
        SLAB[:, i * BLKR : (i + 1) * BLKR] = (W[0:COLS, lanes].astype(F32) * slab_scale[:, i : i + 1]).astype(BF16)
    WS[...] = SLAB[...].T.reshape(NX, 2, ROWS // 2, COLS)
    wx = []
    for r in range(1, NX):
        wx.append(start(copy(WS.at[lax.rem(x + r, NX), core], WX.at[NX - r, y, core], dev_x(r))))

    arrived(qz_c[1])
    qz_c[2] = qz(2)
    q_first(1, 7)
    arrived(px1)
    px2 = x_second(0, QR, QR + PH, ROWS)
    p_next(1, before, "before")
    p_next(1, after, "after")
    p_next(2, x, "own")
    def y_unit(rel):
        return WX.at[1:NX, lax.rem(y + rel, NY), core]

    def y_ring(step):
        if step < 4:
            a = y_unit(NY - step + 1)
            b = y_unit(step - 1)
        else:
            a = WX.at[1:NX, lax.rem(y + 5, NY), core, 0:48]
            b = WX.at[1:NX, lax.rem(y + 3, NY), core, 48:80]
        return start(copy(a, a, dev_y(1))), start(copy(b, b, dev_y(NY - 1)))

    swaps = []

    def core_swap(*places):
        for rel in places:
            a = y_unit(rel)
            swaps.append(start(copy(a, a, other_core)))

    for c in wx:
        c.wait_recv()
    y1 = y_ring(1)
    core_swap(0)
    for c in dx:
        c.wait_recv()
    DN[0] = jnp.concatenate([DX[i, :, 0:ROWS] for i in range(NX)], axis=1)
    dn1 = dn_ring(1)

    load_grad.wait()
    for i in range(32):
        g = GI[:, i * COLS : (i + 1) * COLS].astype(F32)
        last = [g[4 * q : 4 * q + 4, 256:COLS] for q in range(3)]
        side = jnp.concatenate(last + [jnp.zeros((4, 64), F32)], axis=1)
        GM[i % NX, i // NX] = jnp.concatenate([g[:, 0:256], side], axis=0).astype(BF16)
    gx = [start(copy(GM.at[lax.rem(x + r, NX)], A1.at[x], dev_x(r))) for r in range(1, NX)]
    A1[x] = GM[x]

    for b in range(DIMS // BLKR):
        lanes = slice(b * BLKR, (b + 1) * BLKR)
        W[0:COLS, lanes] = (W[0:COLS, lanes].astype(F32) * GS[:, b : b + 1]).astype(BF16)

    q_second(0)
    arrived(qz_c[2])
    qz_c[3] = qz(3)
    q_first(2, 6)
    arrived(px2)
    p_next(1, opposite, "opposite")

    for c in gx:
        c.wait_recv()
    A2[z] = A1[:, z]
    gz = [start(copy(A1.at[:, lax.rem(z + r, NZ)], A2.at[z], dev_z(r))) for r in range(1, NZ)]

    q_second(1, 7)
    p_next(2, before, "before")
    p_next(2, after, "after")
    p_next(3, x, "own")
    arrived(dn1)
    dn2 = dn_ring(2)

    def turn(k):
        WT[...] = W[0:COLS, pl.ds(pl.multiple_of(k * group + x * BLKR, BLKR), 256)].T
        rows = WT[pl.ds(pl.multiple_of(x * 32, 32), ROWS), :]
        WX[0, k] = rows.reshape(2, ROWS // 2, COLS)


    arrived(qz_c[3])
    qz_c[4] = qz(4)
    q_first(3, 5)
    p_next(2, opposite, "opposite")
    q_second(2, 6)
    p_next(3, before, "before")
    p_next(3, after, "after")
    p_next(4, x, "own")
    arrived(dn2)
    dn3 = dn_ring(3)
    for k in range(NZ // 2):
        turn(k)
    arrived(y1)
    y2 = y_ring(2)
    core_swap(1, 7)

    arrived(qz_c[4])
    q_first(4)
    p_next(3, opposite, "opposite")
    q_second(3, 5)
    p_next(4, before, "before")
    p_next(4, after, "after")
    arrived(dn3)
    dn4 = dn_ring(4)
    for c in gz:
        c.wait_recv()
    ga = start(copy(A2.at[pl.ds((1 - sec) * (NZ // 2), NZ // 2)], A3, (dp, t, 1 - sec)))
    for k in range(NZ // 2, NZ):
        turn(k)

    ACC[...] = jnp.zeros_like(ACC)

    def forward(rz):
        if rz == 4:
            for name in ("own", "before", "after", "opposite"):
                arrived(pz_c[name, 4])
        arrived(qx2[rz])
        lanes = w_lanes(lax.rem(z + rz, NZ))
        W[COLS : COLS + RANK, lanes] = DN[rz]
        ACC[...] += dot(W[:, lanes], C[rz * NX : (rz + 1) * NX].reshape(group, CROP))

    q_second(4)
    p_next(4, opposite, "opposite")
    forward(0)
    arrived(y2)
    y3 = y_ring(3)
    core_swap(2, 6)
    forward(1)
    forward(7)

    for c in load_rest:
        c.wait()
    ga.wait_recv()
    residue = MAP[...]
    block = lax.shift_right_logical(residue * 43691, 19)
    row = residue - block * OWNED
    quarter = lax.shift_right_logical(row, 2)
    token = lax.broadcasted_iota(jnp.int32, (1, CROP), 1)
    valid = token < len_ref[0]
    parity = block & 1
    slot = lax.shift_right_logical(block, 1) + jnp.where(parity == sec, 0, 16)
    place = jnp.where(valid, slot * SLOT + row, -1)
    place_last = jnp.where(valid, slot * SLOT + OWNED + (row - quarter * 4), -1)
    index = lax.broadcasted_iota(jnp.int32, (32 * SLOT, CROP), 0)
    mine = A2[pl.ds(sec * (NZ // 2), NZ // 2)].reshape(16 * SLOT, 256)
    rows = jnp.concatenate([mine, A3[...].reshape(16 * SLOT, 256)], axis=0)
    most = dot(rows, (index == place).astype(F32).astype(BF16), ((0,), (0,)))
    last = dot(rows, (index == place_last).astype(F32).astype(BF16), ((0,), (0,)))
    last = jnp.where(quarter == 0, last[0:64], jnp.where(quarter == 1, last[64:128], last[128:192]))
    upstream = jnp.concatenate([most, last], axis=0)
    gain = jnp.broadcast_to(gain_ref[...].astype(F32).reshape(1, COLS), (8, COLS)).T[:, 0:1]
    scaled = gain * upstream

    forward(2)
    forward(6)
    forward(3)
    forward(5)
    arrived(y3)
    y4 = y_ring(4)
    core_swap(3, 5)
    arrived(dn4)
    forward(4)

    inner = ACC[COLS : COLS + RANK, :].astype(BF16)
    hidden = ACC[0:COLS, :] + ADAPTER_SCALE * dot(UP[...], inner, ((0,), (0,))) + RES[...].astype(F32)
    ST[0:1, :] = jnp.sum(hidden, axis=0, keepdims=True)
    ST[1:2, :] = jnp.sum(hidden * hidden, axis=0, keepdims=True)
    ST[2:3, :] = jnp.sum(scaled, axis=0, keepdims=True)
    ST[3:4, :] = jnp.sum(scaled * hidden, axis=0, keepdims=True)
    sx = [start(copy(ST, SX.at[r], dev_x(r))) for r in range(1, NX)]
    for c in sx:
        c.wait_recv()
    SZ[0] = (ST[...] + SX[1]) + (SX[2] + SX[3])
    sz = [start(copy(SZ.at[0], SZ.at[r], dev_z(r))) for r in range(1, NZ)]
    arrived(y4)
    core_swap(4)
    for c in sz:
        c.wait_recv()
    sums = jnp.sum(SZ[...], axis=0) / MODEL_WIDTH
    average = sums[0:1, :]
    variance = sums[1:2, :] - average * average
    inverse = lax.rsqrt(variance + 1e-05)
    first_mean = sums[2:3, :]
    second_mean = inverse * (sums[3:4, :] - average * first_mean)
    normed = (hidden - average) * inverse
    gradient = (inverse * (scaled - first_mean - normed * second_mean)).astype(BF16)
    for b in range(NBLOCK):
        HX[b, 0] = gradient[:, b * TOKEN_BLOCK : (b + 1) * TOKEN_BLOCK]

    def hx_first(b):
        return (
            start(copy(HX.at[b, 0], HX.at[b, 3], dev_x(1))),
            start(copy(HX.at[b, 0], HX.at[b, 1], dev_x(NX - 1))),
        )

    def hx_second(b):
        arrived(h1[b])
        return (
            start(copy(HX.at[b, 3, 0:160], HX.at[b, 2, 0:160], dev_x(1))),
            start(copy(HX.at[b, 1, 160:COLS], HX.at[b, 2, 160:COLS], dev_x(NX - 1))),
        )

    h1 = [hx_first(0)]
    TX[0] = dot(UP[...], gradient)
    tx = [start(copy(TX.at[0], TX.at[r], dev_x(r))) for r in range(1, NX)]
    h1 += [hx_first(1), hx_first(2)]
    HG[...] = gradient
    out_hg = local_copy(HG, hg_out)
    FH[...] = (gain * normed).astype(BF16)
    out_fh = local_copy(FH, fh_out)
    UA[...] = ADAPTER_SCALE * dot(inner, gradient, ((1,), (1,)))
    uc = start(copy(UA, UC, other_core))
    for c in tx:
        c.wait_recv()
    TZ[0] = (TX[0] + TX[1]) + (TX[2] + TX[3])
    tz = [start(copy(TZ.at[0], TZ.at[r], dev_z(r))) for r in range(1, NZ)]
    h2 = [hx_second(0)]
    uc.wait_recv()
    UY[0] = UA[...] + UC[...]
    uy = [start(copy(UY.at[0], UY.at[r], dev_y(r))) for r in range(1, NY)]
    for c in swaps:
        c.wait_recv()
    h2.append(hx_second(1))

    halves = NZ * ROWS // 2

    def partials(b):
        arrived(h2[b])

        @pl.loop(0, 2)
        def _(h):
            total = jnp.zeros((halves, TOKEN_BLOCK), F32)
            for r in range(NX):
                w = WX[r, pl.ds(h * (NZ // 2), NZ // 2)].reshape(halves, COLS)
                total = total + dot(w, HX[b, r])
            PART[b, pl.ds(h * (NZ // 2), NZ // 2)] = total.reshape(NZ // 2, ROWS, TOKEN_BLOCK)

    def part(b, rel):
        return PART[b, lax.rem(z + rel, NZ)]

    HALF = ROWS // 2
    rs = {}

    def rs_step(b, step):
        if step == 1:
            RS[b, 0, 0, 0:HALF] = part(b, 4)[0:HALF].astype(BF16)
            RS[b, 1, 0, 0:HALF] = part(b, 4)[HALF:ROWS].astype(BF16)
            right = copy(RS.at[b, 0, 0, 0:HALF], RR.at[b, 0, 0:HALF], dev_z(1))
            left = copy(RS.at[b, 1, 0, 0:HALF], LR.at[b, 0, 0:HALF], dev_z(NZ - 1))
        else:
            arrived(rs[b, step - 1])
            mine_right, mine_left = part(b, 5 - step), part(b, 3 + step)
            if step == 2:
                RS[b, 0, 1, 0:HALF] = (mine_right[0:HALF] + RR[b, 0, 0:HALF].astype(F32)).astype(BF16)
                RS[b, 0, 1, HALF:ROWS] = mine_right[HALF:ROWS].astype(BF16)
                RS[b, 1, 1, 0:HALF] = mine_left[0:HALF].astype(BF16)
                RS[b, 1, 1, HALF:ROWS] = (mine_left[HALF:ROWS] + LR[b, 0, 0:HALF].astype(F32)).astype(BF16)
            else:
                RS[b, 0, step - 1] = (mine_right + RR[b, step - 2].astype(F32)).astype(BF16)
                RS[b, 1, step - 1] = (mine_left + LR[b, step - 2].astype(F32)).astype(BF16)
            right = copy(RS.at[b, 0, step - 1], RR.at[b, step - 1], dev_z(1))
            left = copy(RS.at[b, 1, step - 1], LR.at[b, step - 1], dev_z(NZ - 1))
        rs[b, step] = (start(right), start(left))

    partials(0)
    rs_step(0, 1)
    h2.append(hx_second(2))
    for c in tz:
        c.wait_recv()
    through_all = jnp.sum(TZ[...], axis=0).astype(BF16)
    DA[...] = ADAPTER_SCALE * dot(through_all, C[x], ((1,), (1,)))
    dc = start(copy(DA, DC, other_core))
    adapter = ADAPTER_SCALE * dot(DIN[...], through_all, ((0,), (0,)))
    rs_step(0, 2)
    partials(1)
    rs_step(1, 1)
    dc.wait_recv()
    DY[0] = DA[...] + DC[...]
    dy = [start(copy(DY.at[0], DY.at[r], dev_y(r))) for r in range(1, NY)]
    rs_step(0, 3)
    rs_step(1, 2)
    partials(2)
    rs_step(2, 1)
    rs_step(0, 4)
    rs_step(1, 3)
    rs_step(2, 2)
    rs_step(1, 4)
    for c in uy:
        c.wait_recv()
    UG[...] = jnp.sum(UY[...], axis=0)
    out_ug = local_copy(UG, ug_out)
    rs_step(2, 3)
    for c in dy:
        c.wait_recv()
    DG[...] = jnp.sum(DY[...], axis=0)
    out_dg = local_copy(DG, dg_out)
    rs_step(2, 4)
    for b in range(NBLOCK):
        arrived(rs[b, 4])
        lanes = slice(b * TOKEN_BLOCK, (b + 1) * TOKEN_BLOCK)
        total = part(b, 0) + RR[b, 3].astype(F32) + LR[b, 3].astype(F32)
        CG[:, lanes] = (total + adapter[:, lanes]).astype(BF16)
    out_cg = local_copy(CG, cg_out)

    for c in pending:
        c.wait_send()

    for c in (out_hg, out_fh, out_ug, out_dg, out_cg):
        c.wait()


def finish(*refs):
    for array, out in zip(refs[:5], refs[5:]):
        out[...] = array[...]


def on_device(grad, context, residual, gain, codes, exponents, down, up, residue_map, lengths):
    vmem = pl.BlockSpec(memory_space=pltpu.VMEM)
    anywhere = pl.BlockSpec(memory_space=pl.ANY)
    shapes = (
        jax.ShapeDtypeStruct((ROWS, CROP), BF16),
        jax.ShapeDtypeStruct((COLS, CROP), BF16),
        jax.ShapeDtypeStruct((RANK, ROWS), F32),
        jax.ShapeDtypeStruct((RANK, COLS), F32),
        jax.ShapeDtypeStruct((COLS, CROP), BF16),
    )
    results = pl.pallas_call(
        kernel,
        out_shape=shapes,
        in_specs=[anywhere] * 3 + [vmem] + [anywhere] * 5 + [pl.BlockSpec(memory_space=pltpu.SMEM)],
        out_specs=[anywhere] * 5,
        scratch_shapes=[
            pltpu.VMEM((COLS + RANK, DIMS), BF16),
            pltpu.VMEM((NX * NZ, ROWS, CROP), BF16),
            pltpu.VMEM((NX, RANK, 256), BF16),
            pltpu.VMEM((NZ, RANK, NX * ROWS), BF16),
            pltpu.VMEM((COLS, NX * ROWS), BF16),
            pltpu.VMEM((NX, 2, ROWS // 2, COLS), BF16),
            pltpu.VMEM((256, COLS), BF16),
            pltpu.VMEM((NX, NZ, 2, ROWS // 2, COLS), BF16),
            pltpu.VMEM((OWNED, MODEL_WIDTH), BF16),
            pltpu.VMEM((NX, NZ, SLOT, 256), BF16),
            pltpu.VMEM((NX, NZ, SLOT, 256), BF16),
            pltpu.VMEM((NZ, NX, SLOT, 256), BF16),
            pltpu.VMEM((NZ // 2, NX, SLOT, 256), BF16),
            pltpu.VMEM((COLS + RANK, CROP), F32),
            pltpu.VMEM((NBLOCK, NX, COLS, TOKEN_BLOCK), BF16),
            pltpu.VMEM((NBLOCK, NZ, ROWS, TOKEN_BLOCK), F32),
            pltpu.VMEM((NBLOCK, 2, 4, ROWS, TOKEN_BLOCK), BF16),
            pltpu.VMEM((NBLOCK, 4, ROWS, TOKEN_BLOCK), BF16),
            pltpu.VMEM((NBLOCK, 4, ROWS, TOKEN_BLOCK), BF16),
            pltpu.VMEM((4, CROP), F32),
            pltpu.VMEM((NX, 4, CROP), F32),
            pltpu.VMEM((NZ, 4, CROP), F32),
            pltpu.VMEM((NX, RANK, CROP), F32),
            pltpu.VMEM((NZ, RANK, CROP), F32),
            pltpu.VMEM((RANK, COLS), F32),
            pltpu.VMEM((RANK, COLS), F32),
            pltpu.VMEM((NY, RANK, COLS), F32),
            pltpu.VMEM((RANK, ROWS), F32),
            pltpu.VMEM((RANK, ROWS), F32),
            pltpu.VMEM((NY, RANK, ROWS), F32),
            pltpu.VMEM((COLS, DIMS // BLKR), F32),
            pltpu.VMEM((COLS, CROP), BF16),
            pltpu.VMEM((COLS // BLKC, DIMS // BLKR), jnp.int32),
            pltpu.VMEM((RANK, ROWS), BF16),
            pltpu.VMEM((RANK, COLS), BF16),
            pltpu.VMEM((1, CROP), jnp.int32),
            pltpu.VMEM((ROWS, CROP), BF16),
            pltpu.VMEM((COLS, CROP), BF16),
            pltpu.VMEM((RANK, ROWS), F32),
            pltpu.VMEM((RANK, COLS), F32),
            pltpu.VMEM((COLS, CROP), BF16),
            pltpu.SemaphoreType.DMA((SENDS,)),
            pltpu.SemaphoreType.DMA((SENDS,)),
            pltpu.SemaphoreType.DMA((16,)),
        ],
        compiler_params=pltpu.CompilerParams(
            collective_id=0, has_side_effects=True, vmem_limit_bytes=56 * 1024 * 1024
        ),
        cost_estimate=pl.CostEstimate(flops=2 * 2 * CROP * DIMS * COLS, bytes_accessed=8 << 20, transcendentals=0),
    )(grad, context.T, residual.T, gain, codes.T, exponents.T, down.T, up, residue_map, lengths)
    cg, hg, dg, ug, fh = pl.pallas_call(
        finish,
        out_shape=shapes,
        in_specs=[vmem] * 5,
        out_specs=[vmem] * 5,
    )(*results)
    return cg, hg.T, dg.T, ug, fh.T


def solution(mesh):
    in_specs = (
        P(("dp", "tensor", "section"), None),
        P(("dp", "section"), "tensor"),
        P(("dp", "section"), "tensor"),
        P("tensor"),
        P(None, "tensor"),
        P(None, "tensor"),
        P("tensor", None),
        P(None, "tensor"),
        P(("dp", "section"), None),
        P(("dp", "section")),
    )
    out_specs = (
        P("tensor", ("dp", "section")),
        P(("dp", "section"), "tensor"),
        P("tensor", None),
        P(None, "tensor"),
        P(("dp", "section"), "tensor"),
    )
    return jax.shard_map(
        on_device, mesh=mesh, in_specs=in_specs, out_specs=out_specs, check_vma=False
    )
```

```python
import functools

import jax
import jax.numpy as jnp
from jax import lax
from jax.experimental import pallas as pl
from jax.experimental.pallas import tpu as pltpu
from jax.sharding import PartitionSpec as P

MODEL_WIDTH = 10240
DIMS = 5120
ADAPTER_SCALE = 2.0
CROP = 384
COLS = 320
ROWS = 160
RANK = 16
NX = 4
NZ = 8
NY = 8
BLKR = 128
BLKC = 64
OWNED = 12
SLOT = 16
F32 = jnp.float32
BF16 = jnp.bfloat16
MESH = pl.DeviceIdType.MESH
QR = 96
PH = 32
TOKEN_BLOCK = 128
NBLOCK = CROP // TOKEN_BLOCK

SENDS = 256


def dot(a, b, dims=((1,), (0,))):
    return lax.dot_general(a, b, (dims, ((), ())), preferred_element_type=F32)


def kernel(
    grad_hbm, ctx_hbm, res_hbm, gain_ref, codes_hbm, exp_hbm, down_hbm, up_hbm, map_hbm, len_ref,
    cg_out, hg_out, dg_out, ug_out, fh_out,
    W, C, DX, DN, SLAB, WS, WT, WX, GI, GM, A1, A2, AM, A3, ACC, HX, PART, RS, RR, LR, ST, SX, SZ, TX, TZ,
    UA, UC, UY, DA, DC, DY, GS, RES, EXP, DIN, UP, MAP, CG, HG, DG, UG, FH,
    send_sem, recv_sem, load_sem,
):
    dp = lax.axis_index("dp")
    t = lax.axis_index("tensor")
    sec = lax.axis_index("section")
    x = lax.rem(t, NX)
    z = lax.div(t, NX)
    core = lax.rem(dp, 2)
    y = sec * (NY // 2) + lax.div(dp, 2)

    def dev_x(r):
        return (dp, z * NX + lax.rem(x + r, NX), sec)

    def dev_z(r):
        return (dp, lax.rem(z + r, NZ) * NX + x, sec)

    def dev_y(r):
        other = lax.rem(y + r, NY)
        return (lax.rem(other, NY // 2) * 2 + core, t, lax.div(other, NY // 2))

    other_core = (dp + 1 - 2 * core, t, sec)
    before, after, opposite = lax.rem(x + 3, NX), lax.rem(x + 1, NX), lax.rem(x + 2, NX)

    group = NX * ROWS

    def w_lanes(index):
        return pl.ds(pl.multiple_of(index * group, 128), group)

    local_copies = [0]

    def local_copy(src, dst):
        k = local_copies[0]
        local_copies[0] += 1
        c = pltpu.make_async_copy(src, dst, load_sem.at[k])
        c.start()
        return c

    load_ctx = local_copy(ctx_hbm, C.at[x])
    load_grad = local_copy(grad_hbm, GI)
    load_down = local_copy(down_hbm, DIN)
    load_exp = local_copy(exp_hbm, EXP)
    load_codes = local_copy(codes_hbm, W.at[0:COLS])
    load_rest = [local_copy(map_hbm, MAP), local_copy(up_hbm, UP), local_copy(res_hbm, RES)]

    barrier = pltpu.get_barrier_semaphore()

    def greet(device):
        pl.semaphore_signal(barrier, inc=1, device_id=device, device_id_type=MESH)

    for r in range(1, NX):
        greet(dev_x(r))
    for r in range(1, NZ):
        greet(dev_z(r))
    for r in range(1, NY):
        greet(dev_y(r))
    greet(other_core)

    counter = [0]

    def copy(src, dst, device):
        k = counter[0]
        counter[0] += 1
        return pltpu.make_async_remote_copy(
            src_ref=src, dst_ref=dst, send_sem=send_sem.at[k], recv_sem=recv_sem.at[k],
            device_id=device, device_id_type=MESH,
        )

    pending = []

    def start(c):
        c.start()
        pending.append(c)
        return c

    def arrived(pair):
        for c in pair:
            c.wait_recv()

    load_down.wait()
    DX[x] = jnp.concatenate([DIN[...], jnp.zeros((RANK, 96), BF16)], axis=1)
    load_ctx.wait()

    pl.semaphore_wait(barrier, (NX - 1) + (NZ - 1) + (NY - 1) + 1)

    def z_ring(step, column, lo, mid, hi):
        if step < 4:
            right = copy(
                C.at[((NZ - step + 1) % NZ) * NX + column, lo:hi], C.at[(NZ - step) * NX + column, lo:hi], dev_z(1)
            )
            left = copy(C.at[(step - 1) * NX + column, lo:hi], C.at[step * NX + column, lo:hi], dev_z(NZ - 1))
        else:
            right = copy(C.at[5 * NX + column, lo:mid], C.at[4 * NX + column, lo:mid], dev_z(1))
            left = copy(C.at[3 * NX + column, mid:hi], C.at[4 * NX + column, mid:hi], dev_z(NZ - 1))
        return start(right), start(left)

    def qz(step):
        return z_ring(step, x, 0, 48, QR)

    def pz(step, column):
        return z_ring(step, column, QR, QR + PH, ROWS)

    def x_first(rz, lo, hi):
        own = C.at[rz * NX + x, lo:hi]
        return start(copy(own, own, dev_x(1))), start(copy(own, own, dev_x(NX - 1)))

    def x_second(rz, lo, mid, hi):
        a = C.at[rz * NX + before, lo:mid]
        b = C.at[rz * NX + after, mid:hi]
        return start(copy(a, a, dev_x(1))), start(copy(b, b, dev_x(NX - 1)))

    qz_c, qx1, qx2, pz_c = {}, {}, {}, {}

    def q_first(*places):
        for rz in places:
            qx1[rz] = x_first(rz, 0, QR)

    def q_second(*places):
        for rz in places:
            arrived(qx1[rz])
            qx2[rz] = x_second(rz, 0, 48, QR)

    def p_next(step, column, name):
        if step > 1:
            arrived(pz_c[name, step - 1])
        pz_c[name, step] = pz(step, column)

    def dn_ring(step):
        if step < 4:
            right = copy(DN.at[(NZ - step + 1) % NZ], DN.at[NZ - step], dev_z(1))
            left = copy(DN.at[step - 1], DN.at[step], dev_z(NZ - 1))
            return start(right), start(left)
        return (start(copy(DN.at[5], DN.at[4], dev_z(1))),)

    qz_c[1] = qz(1)
    px1 = x_first(0, QR, ROWS)
    dx = [start(copy(DX.at[x], DX.at[x], dev_x(r))) for r in range(1, NX)]
    p_next(1, x, "own")
    q_first(0)

    load_exp.wait()
    codes_scale = EXP[...]
    factor = jnp.where(
        codes_scale == -3, 0.125,
        jnp.where(codes_scale == -2, 0.25, jnp.where(codes_scale == -1, 0.5, jnp.where(codes_scale == 0, 1.0, 2.0))),
    ).astype(F32)
    for j in range(COLS // BLKC):
        GS[j * BLKC : (j + 1) * BLKC, :] = jnp.broadcast_to(factor[j : j + 1, :], (BLKC, DIMS // BLKR))
    load_codes.wait()

    picked = (
        lax.broadcasted_iota(jnp.int32, (DIMS // BLKR, 128), 0)
        == y * (group // BLKR) + lax.broadcasted_iota(jnp.int32, (DIMS // BLKR, 128), 1)
    )
    slab_scale = dot(GS[...].astype(BF16), picked.astype(F32).astype(BF16))
    for i in range(group // BLKR):
        lanes = pl.ds(pl.multiple_of(y * group + i * BLKR, BLKR), BLKR)
        SLAB[:, i * BLKR : (i + 1) * BLKR] = (W[0:COLS, lanes].astype(F32) * slab_scale[:, i : i + 1]).astype(BF16)
    WS[...] = SLAB[...].T.reshape(NX, 2, ROWS // 2, COLS)
    wx = []
    for r in range(1, NX):
        wx.append(start(copy(WS.at[lax.rem(x + r, NX), core], WX.at[NX - r, y, core], dev_x(r))))

    load_grad.wait()
    for i in range(32):
        g = GI[:, i * COLS : (i + 1) * COLS].astype(F32)
        last = [g[4 * q : 4 * q + 4, 256:COLS] for q in range(3)]
        side = jnp.concatenate(last + [jnp.zeros((4, 64), F32)], axis=1)
        GM[i % NX, i // NX] = jnp.concatenate([g[:, 0:256], side], axis=0).astype(BF16)
    gx = [start(copy(GM.at[lax.rem(x + r, NX)], A1.at[x], dev_x(r))) for r in range(1, NX)]
    A1[x] = GM[x]

    arrived(qz_c[1])
    qz_c[2] = qz(2)
    q_first(1, 7)
    arrived(px1)
    px2 = x_second(0, QR, QR + PH, ROWS)
    p_next(1, before, "before")
    p_next(1, after, "after")
    p_next(2, x, "own")
    def y_unit(rel):
        return WX.at[1:NX, lax.rem(y + rel, NY), core]

    y_c = {}

    def y_ring(step):
        for r in range(1, NX):
            if step > 1:
                arrived(y_c[r, step - 1])
            if step < 4:
                a = WX.at[r, lax.rem(y + NY - step + 1, NY), core]
                b = WX.at[r, lax.rem(y + step - 1, NY), core]
            else:
                a = WX.at[r, lax.rem(y + 5, NY), core, 0:48]
                b = WX.at[r, lax.rem(y + 3, NY), core, 48:80]
            y_c[r, step] = (start(copy(a, a, dev_y(1))), start(copy(b, b, dev_y(NY - 1))))

    swaps = []

    def core_swap(*places):
        for rel in places:
            a = y_unit(rel)
            swaps.append(start(copy(a, a, other_core)))

    for c in wx:
        c.wait_recv()
    y_ring(1)
    core_swap(0)
    for c in dx:
        c.wait_recv()
    DN[0] = jnp.concatenate([DX[i, :, 0:ROWS] for i in range(NX)], axis=1)
    dn1 = dn_ring(1)
    for c in gx:
        c.wait_recv()
    A2[z] = A1[:, z]
    gz = [start(copy(A1.at[:, lax.rem(z + r, NZ)], A2.at[z], dev_z(r))) for r in range(1, NZ)]

    for b in range(DIMS // BLKR):
        lanes = slice(b * BLKR, (b + 1) * BLKR)
        W[0:COLS, lanes] = (W[0:COLS, lanes].astype(F32) * GS[:, b : b + 1]).astype(BF16)

    q_second(0)
    arrived(qz_c[2])
    qz_c[3] = qz(3)
    q_first(2, 6)
    arrived(px2)
    p_next(1, opposite, "opposite")
    for c in gz:
        c.wait_recv()
    away = (1 - sec) * (NZ // 2)
    am = (
        start(copy(A2.at[pl.ds(away, 2)], AM.at[0], dev_y(2))),
        start(copy(A2.at[pl.ds(away + 2, 2)], AM.at[1], dev_y(NY - 2))),
    )

    q_second(1, 7)
    p_next(2, before, "before")
    p_next(2, after, "after")
    p_next(3, x, "own")
    arrived(dn1)
    dn2 = dn_ring(2)
    y_ring(2)
    core_swap(1, 7)
    arrived(am)
    ga = (start(copy(AM.at[0], A3.at[0:2], dev_y(2))), start(copy(AM.at[1], A3.at[2:4], dev_y(NY - 2))))

    def turn(k):
        WT[...] = W[0:COLS, pl.ds(pl.multiple_of(k * group + x * BLKR, BLKR), 256)].T
        rows = WT[pl.ds(pl.multiple_of(x * 32, 32), ROWS), :]
        WX[0, k] = rows.reshape(2, ROWS // 2, COLS)


    arrived(qz_c[3])
    qz_c[4] = qz(4)
    q_first(3, 5)
    p_next(2, opposite, "opposite")
    q_second(2, 6)
    p_next(3, before, "before")
    p_next(3, after, "after")
    p_next(4, x, "own")
    arrived(dn2)
    dn3 = dn_ring(3)
    y_ring(3)
    core_swap(2, 6)
    for k in range(NZ // 2):
        turn(k)

    arrived(qz_c[4])
    q_first(4)
    p_next(3, opposite, "opposite")
    q_second(3, 5)
    p_next(4, before, "before")
    p_next(4, after, "after")
    arrived(dn3)
    dn4 = dn_ring(4)
    y_ring(4)
    core_swap(3, 5)
    for k in range(NZ // 2, NZ):
        turn(k)

    ACC[...] = jnp.zeros_like(ACC)

    def forward(rz):
        if rz == 4:
            for name in ("own", "before", "after", "opposite"):
                arrived(pz_c[name, 4])
        arrived(qx2[rz])
        lanes = w_lanes(lax.rem(z + rz, NZ))
        W[COLS : COLS + RANK, lanes] = DN[rz]
        ACC[...] += dot(W[:, lanes], C[rz * NX : (rz + 1) * NX].reshape(group, CROP))

    q_second(4)
    p_next(4, opposite, "opposite")
    forward(0)
    forward(1)
    forward(7)

    for c in load_rest:
        c.wait()
    arrived(ga)
    residue = MAP[...]
    block = lax.shift_right_logical(residue * 43691, 19)
    row = residue - block * OWNED
    quarter = lax.shift_right_logical(row, 2)
    token = lax.broadcasted_iota(jnp.int32, (1, CROP), 1)
    valid = token < len_ref[0]
    parity = block & 1
    slot = lax.shift_right_logical(block, 1) + jnp.where(parity == sec, 0, 16)
    place = jnp.where(valid, slot * SLOT + row, -1)
    place_last = jnp.where(valid, slot * SLOT + OWNED + (row - quarter * 4), -1)
    index = lax.broadcasted_iota(jnp.int32, (32 * SLOT, CROP), 0)
    mine = A2[pl.ds(sec * (NZ // 2), NZ // 2)].reshape(16 * SLOT, 256)
    rows = jnp.concatenate([mine, A3[...].reshape(16 * SLOT, 256)], axis=0)
    most = dot(rows, (index == place).astype(F32).astype(BF16), ((0,), (0,)))
    last = dot(rows, (index == place_last).astype(F32).astype(BF16), ((0,), (0,)))
    last = jnp.where(quarter == 0, last[0:64], jnp.where(quarter == 1, last[64:128], last[128:192]))
    upstream = jnp.concatenate([most, last], axis=0)
    gain = jnp.broadcast_to(gain_ref[...].astype(F32).reshape(1, COLS), (8, COLS)).T[:, 0:1]
    scaled = gain * upstream

    forward(2)
    forward(6)
    forward(3)
    forward(5)
    arrived(dn4)
    forward(4)

    inner = ACC[COLS : COLS + RANK, :].astype(BF16)
    hidden = ACC[0:COLS, :] + ADAPTER_SCALE * dot(UP[...], inner, ((0,), (0,))) + RES[...].astype(F32)
    ST[0:1, :] = jnp.sum(hidden, axis=0, keepdims=True)
    ST[1:2, :] = jnp.sum(hidden * hidden, axis=0, keepdims=True)
    ST[2:3, :] = jnp.sum(scaled, axis=0, keepdims=True)
    ST[3:4, :] = jnp.sum(scaled * hidden, axis=0, keepdims=True)
    sx = [start(copy(ST, SX.at[r], dev_x(r))) for r in range(1, NX)]
    for c in sx:
        c.wait_recv()
    SZ[0] = (ST[...] + SX[1]) + (SX[2] + SX[3])
    sz = [start(copy(SZ.at[0], SZ.at[r], dev_z(r))) for r in range(1, NZ)]
    for r in range(1, NX):
        arrived(y_c[r, 4])
    core_swap(4)
    for c in sz:
        c.wait_recv()
    sums = jnp.sum(SZ[...], axis=0) / MODEL_WIDTH
    average = sums[0:1, :]
    variance = sums[1:2, :] - average * average
    inverse = lax.rsqrt(variance + 1e-05)
    first_mean = sums[2:3, :]
    second_mean = inverse * (sums[3:4, :] - average * first_mean)
    normed = (hidden - average) * inverse
    gradient = (inverse * (scaled - first_mean - normed * second_mean)).astype(BF16)
    for b in range(NBLOCK):
        HX[b, 0] = gradient[:, b * TOKEN_BLOCK : (b + 1) * TOKEN_BLOCK]

    def hx_first(b):
        return (
            start(copy(HX.at[b, 0], HX.at[b, 3], dev_x(1))),
            start(copy(HX.at[b, 0], HX.at[b, 1], dev_x(NX - 1))),
        )

    def hx_second(b):
        arrived(h1[b])
        return (
            start(copy(HX.at[b, 3, 0:160], HX.at[b, 2, 0:160], dev_x(1))),
            start(copy(HX.at[b, 1, 160:COLS], HX.at[b, 2, 160:COLS], dev_x(NX - 1))),
        )

    h1 = [hx_first(0)]
    TX[0] = dot(UP[...], gradient)
    tx = [start(copy(TX.at[0], TX.at[r], dev_x(r))) for r in range(1, NX)]
    h1 += [hx_first(1), hx_first(2)]
    HG[...] = gradient
    out_hg = local_copy(HG, hg_out)
    FH[...] = (gain * normed).astype(BF16)
    out_fh = local_copy(FH, fh_out)
    UA[...] = ADAPTER_SCALE * dot(inner, gradient, ((1,), (1,)))
    uc = start(copy(UA, UC, other_core))
    for c in tx:
        c.wait_recv()
    TZ[0] = (TX[0] + TX[1]) + (TX[2] + TX[3])
    tz = [start(copy(TZ.at[0], TZ.at[r], dev_z(r))) for r in range(1, NZ)]
    h2 = [hx_second(0)]
    uc.wait_recv()
    UY[0] = UA[...] + UC[...]
    uy = [start(copy(UY.at[0], UY.at[r], dev_y(r))) for r in range(1, NY)]
    for c in swaps:
        c.wait_recv()
    h2.append(hx_second(1))

    halves = NZ * ROWS // 2

    def partials(b):
        arrived(h2[b])

        @pl.loop(0, 2)
        def _(h):
            total = jnp.zeros((halves, TOKEN_BLOCK), F32)
            for r in range(NX):
                w = WX[r, pl.ds(h * (NZ // 2), NZ // 2)].reshape(halves, COLS)
                total = total + dot(w, HX[b, r])
            PART[b, pl.ds(h * (NZ // 2), NZ // 2)] = total.reshape(NZ // 2, ROWS, TOKEN_BLOCK)

    def part(b, rel):
        return PART[b, lax.rem(z + rel, NZ)]

    HALF = ROWS // 2
    rs = {}

    def rs_step(b, step):
        if step == 1:
            RS[b, 0, 0, 0:HALF] = part(b, 4)[0:HALF].astype(BF16)
            RS[b, 1, 0, 0:HALF] = part(b, 4)[HALF:ROWS].astype(BF16)
            right = copy(RS.at[b, 0, 0, 0:HALF], RR.at[b, 0, 0:HALF], dev_z(1))
            left = copy(RS.at[b, 1, 0, 0:HALF], LR.at[b, 0, 0:HALF], dev_z(NZ - 1))
        else:
            arrived(rs[b, step - 1])
            mine_right, mine_left = part(b, 5 - step), part(b, 3 + step)
            if step == 2:
                RS[b, 0, 1, 0:HALF] = (mine_right[0:HALF] + RR[b, 0, 0:HALF].astype(F32)).astype(BF16)
                RS[b, 0, 1, HALF:ROWS] = mine_right[HALF:ROWS].astype(BF16)
                RS[b, 1, 1, 0:HALF] = mine_left[0:HALF].astype(BF16)
                RS[b, 1, 1, HALF:ROWS] = (mine_left[HALF:ROWS] + LR[b, 0, 0:HALF].astype(F32)).astype(BF16)
            else:
                RS[b, 0, step - 1] = (mine_right + RR[b, step - 2].astype(F32)).astype(BF16)
                RS[b, 1, step - 1] = (mine_left + LR[b, step - 2].astype(F32)).astype(BF16)
            right = copy(RS.at[b, 0, step - 1], RR.at[b, step - 1], dev_z(1))
            left = copy(RS.at[b, 1, step - 1], LR.at[b, step - 1], dev_z(NZ - 1))
        rs[b, step] = (start(right), start(left))

    def rs_short(b, step):
        if step == 1:
            for side, three in ((0, 3), (1, 5)):
                lo, hi = (0, HALF) if side == 0 else (HALF, ROWS)
                RS[b, side, 0, 0:HALF] = part(b, 4)[lo:hi].astype(BF16)
                RS[b, side, 1] = part(b, three).astype(BF16)
            rs[b, 1] = (
                start(copy(RS.at[b, 0, 0, 0:HALF], RR.at[b, 0, 0:HALF], dev_z(2))),
                start(copy(RS.at[b, 1, 0, 0:HALF], LR.at[b, 0, 0:HALF], dev_z(NZ - 2))),
                start(copy(RS.at[b, 0, 1], RR.at[b, 1], dev_z(1))),
                start(copy(RS.at[b, 1, 1], LR.at[b, 1], dev_z(NZ - 1))),
            )
            RS[b, 0, 2] = part(b, 1).astype(BF16)
            RS[b, 1, 2] = part(b, 7).astype(BF16)
            rs[b, 4] = (
                start(copy(RS.at[b, 0, 2], RR.at[b, 2], dev_z(1))),
                start(copy(RS.at[b, 1, 2], LR.at[b, 2], dev_z(NZ - 1))),
            )
        else:
            arrived(rs[b, 1])
            right = part(b, 2) + RR[b, 1].astype(F32)
            left = part(b, 6) + LR[b, 1].astype(F32)
            RS[b, 0, 3, 0:HALF] = (right[0:HALF] + RR[b, 0, 0:HALF].astype(F32)).astype(BF16)
            RS[b, 0, 3, HALF:ROWS] = right[HALF:ROWS].astype(BF16)
            RS[b, 1, 3, 0:HALF] = left[0:HALF].astype(BF16)
            RS[b, 1, 3, HALF:ROWS] = (left[HALF:ROWS] + LR[b, 0, 0:HALF].astype(F32)).astype(BF16)
            rs[b, 4] += (
                start(copy(RS.at[b, 0, 3], RR.at[b, 3], dev_z(2))),
                start(copy(RS.at[b, 1, 3], LR.at[b, 3], dev_z(NZ - 2))),
            )

    partials(0)
    rs_step(0, 1)
    h2.append(hx_second(2))
    for c in tz:
        c.wait_recv()
    through_all = jnp.sum(TZ[...], axis=0).astype(BF16)
    DA[...] = ADAPTER_SCALE * dot(through_all, C[x], ((1,), (1,)))
    dc = start(copy(DA, DC, other_core))
    adapter = ADAPTER_SCALE * dot(DIN[...], through_all, ((0,), (0,)))
    rs_step(0, 2)
    partials(1)
    rs_step(1, 1)
    dc.wait_recv()
    DY[0] = DA[...] + DC[...]
    dy = [start(copy(DY.at[0], DY.at[r], dev_y(r))) for r in range(1, NY)]
    rs_step(0, 3)
    rs_step(1, 2)
    partials(2)
    rs_short(2, 1)
    rs_step(0, 4)
    rs_step(1, 3)
    rs_short(2, 2)
    rs_step(1, 4)
    for c in uy:
        c.wait_recv()
    UG[...] = jnp.sum(UY[...], axis=0)
    out_ug = local_copy(UG, ug_out)
    for c in dy:
        c.wait_recv()
    DG[...] = jnp.sum(DY[...], axis=0)
    out_dg = local_copy(DG, dg_out)
    for b in range(NBLOCK):
        arrived(rs[b, 4])
        lanes = slice(b * TOKEN_BLOCK, (b + 1) * TOKEN_BLOCK)
        total = part(b, 0) + RR[b, 3].astype(F32) + LR[b, 3].astype(F32)
        if b == NBLOCK - 1:
            total = total + RR[b, 2].astype(F32) + LR[b, 2].astype(F32)
        CG[:, lanes] = (total + adapter[:, lanes]).astype(BF16)
    out_cg = local_copy(CG, cg_out)

    for c in pending:
        c.wait_send()

    for c in (out_hg, out_fh, out_ug, out_dg, out_cg):
        c.wait()


def finish(*refs):
    arrays, outs, held, sems = refs[:5], refs[5:10], refs[10:15], refs[15]
    loads = [pltpu.make_async_copy(a, h, sems.at[0, i]) for i, (a, h) in enumerate(zip(arrays, held))]
    stores = [pltpu.make_async_copy(h, o, sems.at[1, i]) for i, (h, o) in enumerate(zip(held, outs))]
    for c in loads:
        c.start()
    for load, store in zip(loads, stores):
        load.wait()
        store.start()
    for c in stores:
        c.wait()


def on_device(grad, context, residual, gain, codes, exponents, down, up, residue_map, lengths):
    vmem = pl.BlockSpec(memory_space=pltpu.VMEM)
    anywhere = pl.BlockSpec(memory_space=pl.ANY)
    shapes = (
        jax.ShapeDtypeStruct((ROWS, CROP), BF16),
        jax.ShapeDtypeStruct((COLS, CROP), BF16),
        jax.ShapeDtypeStruct((RANK, ROWS), F32),
        jax.ShapeDtypeStruct((RANK, COLS), F32),
        jax.ShapeDtypeStruct((COLS, CROP), BF16),
    )
    results = pl.pallas_call(
        kernel,
        out_shape=shapes,
        in_specs=[anywhere] * 3 + [vmem] + [anywhere] * 5 + [pl.BlockSpec(memory_space=pltpu.SMEM)],
        out_specs=[anywhere] * 5,
        scratch_shapes=[
            pltpu.VMEM((COLS + RANK, DIMS), BF16),
            pltpu.VMEM((NX * NZ, ROWS, CROP), BF16),
            pltpu.VMEM((NX, RANK, 256), BF16),
            pltpu.VMEM((NZ, RANK, NX * ROWS), BF16),
            pltpu.VMEM((COLS, NX * ROWS), BF16),
            pltpu.VMEM((NX, 2, ROWS // 2, COLS), BF16),
            pltpu.VMEM((256, COLS), BF16),
            pltpu.VMEM((NX, NZ, 2, ROWS // 2, COLS), BF16),
            pltpu.VMEM((OWNED, MODEL_WIDTH), BF16),
            pltpu.VMEM((NX, NZ, SLOT, 256), BF16),
            pltpu.VMEM((NX, NZ, SLOT, 256), BF16),
            pltpu.VMEM((NZ, NX, SLOT, 256), BF16),
            pltpu.VMEM((2, 2, NX, SLOT, 256), BF16),
            pltpu.VMEM((NZ // 2, NX, SLOT, 256), BF16),
            pltpu.VMEM((COLS + RANK, CROP), F32),
            pltpu.VMEM((NBLOCK, NX, COLS, TOKEN_BLOCK), BF16),
            pltpu.VMEM((NBLOCK, NZ, ROWS, TOKEN_BLOCK), F32),
            pltpu.VMEM((NBLOCK, 2, 4, ROWS, TOKEN_BLOCK), BF16),
            pltpu.VMEM((NBLOCK, 4, ROWS, TOKEN_BLOCK), BF16),
            pltpu.VMEM((NBLOCK, 4, ROWS, TOKEN_BLOCK), BF16),
            pltpu.VMEM((4, CROP), F32),
            pltpu.VMEM((NX, 4, CROP), F32),
            pltpu.VMEM((NZ, 4, CROP), F32),
            pltpu.VMEM((NX, RANK, CROP), F32),
            pltpu.VMEM((NZ, RANK, CROP), F32),
            pltpu.VMEM((RANK, COLS), F32),
            pltpu.VMEM((RANK, COLS), F32),
            pltpu.VMEM((NY, RANK, COLS), F32),
            pltpu.VMEM((RANK, ROWS), F32),
            pltpu.VMEM((RANK, ROWS), F32),
            pltpu.VMEM((NY, RANK, ROWS), F32),
            pltpu.VMEM((COLS, DIMS // BLKR), F32),
            pltpu.VMEM((COLS, CROP), BF16),
            pltpu.VMEM((COLS // BLKC, DIMS // BLKR), jnp.int32),
            pltpu.VMEM((RANK, ROWS), BF16),
            pltpu.VMEM((RANK, COLS), BF16),
            pltpu.VMEM((1, CROP), jnp.int32),
            pltpu.VMEM((ROWS, CROP), BF16),
            pltpu.VMEM((COLS, CROP), BF16),
            pltpu.VMEM((RANK, ROWS), F32),
            pltpu.VMEM((RANK, COLS), F32),
            pltpu.VMEM((COLS, CROP), BF16),
            pltpu.SemaphoreType.DMA((SENDS,)),
            pltpu.SemaphoreType.DMA((SENDS,)),
            pltpu.SemaphoreType.DMA((16,)),
        ],
        compiler_params=pltpu.CompilerParams(
            collective_id=0, has_side_effects=True, vmem_limit_bytes=56 * 1024 * 1024
        ),
        cost_estimate=pl.CostEstimate(flops=2 * 2 * CROP * DIMS * COLS, bytes_accessed=8 << 20, transcendentals=0),
    )(grad, context.T, residual.T, gain, codes.T, exponents.T, down.T, up, residue_map, lengths)
    cg, hg, dg, ug, fh = pl.pallas_call(
        finish,
        out_shape=shapes,
        in_specs=[anywhere] * 5,
        out_specs=[anywhere] * 5,
        scratch_shapes=[pltpu.VMEM(a.shape, a.dtype) for a in shapes] + [pltpu.SemaphoreType.DMA((2, 5))],
    )(*results)
    return cg, hg.T, dg.T, ug, fh.T


def solution(mesh):
    in_specs = (
        P(("dp", "tensor", "section"), None),
        P(("dp", "section"), "tensor"),
        P(("dp", "section"), "tensor"),
        P("tensor"),
        P(None, "tensor"),
        P(None, "tensor"),
        P("tensor", None),
        P(None, "tensor"),
        P(("dp", "section"), None),
        P(("dp", "section")),
    )
    out_specs = (
        P("tensor", ("dp", "section")),
        P(("dp", "section"), "tensor"),
        P("tensor", None),
        P(None, "tensor"),
        P(("dp", "section"), "tensor"),
    )
    return jax.shard_map(
        on_device, mesh=mesh, in_specs=in_specs, out_specs=out_specs, check_vma=False
    )
```

```python
import functools

import jax
import jax.numpy as jnp
from jax import lax
from jax.experimental import pallas as pl
from jax.experimental.pallas import tpu as pltpu
from jax.sharding import PartitionSpec as P

MODEL_WIDTH = 10240
DIMS = 5120
ADAPTER_SCALE = 2.0
CROP = 384
COLS = 320
ROWS = 160
RANK = 16
NX = 4
NZ = 8
NY = 8
BLKR = 128
BLKC = 64
OWNED = 12
SLOT = 16
F32 = jnp.float32
BF16 = jnp.bfloat16
MESH = pl.DeviceIdType.MESH
QR = 96
PH = 32
TOKEN_BLOCK = 128
NBLOCK = CROP // TOKEN_BLOCK

SENDS = 256


def dot(a, b, dims=((1,), (0,))):
    return lax.dot_general(a, b, (dims, ((), ())), preferred_element_type=F32)


def kernel(
    grad_hbm, ctx_hbm, res_hbm, gain_ref, codes_hbm, exp_hbm, down_hbm, up_hbm, map_hbm, len_ref,
    cg_out, hg_out, dg_out, ug_out, fh_out,
    W, C, DX, DN, SLAB, WS, WT, WX, GI, GM, A1, A2, AM, A3, ACC, HX, PART, RS, RR, LR, ST, SX, SZ, TX, TZ,
    UA, UC, UY, DA, DC, DY, GS, RES, EXP, DIN, UP, MAP, CG, HG, DG, UG, FH,
    send_sem, recv_sem, load_sem,
):
    dp = lax.axis_index("dp")
    t = lax.axis_index("tensor")
    sec = lax.axis_index("section")
    x = lax.rem(t, NX)
    z = lax.div(t, NX)
    core = lax.rem(dp, 2)
    y = sec * (NY // 2) + lax.div(dp, 2)

    def dev_x(r):
        return (dp, z * NX + lax.rem(x + r, NX), sec)

    def dev_z(r):
        return (dp, lax.rem(z + r, NZ) * NX + x, sec)

    def dev_y(r):
        other = lax.rem(y + r, NY)
        return (lax.rem(other, NY // 2) * 2 + core, t, lax.div(other, NY // 2))

    other_core = (dp + 1 - 2 * core, t, sec)
    before, after, opposite = lax.rem(x + 3, NX), lax.rem(x + 1, NX), lax.rem(x + 2, NX)

    group = NX * ROWS

    def w_lanes(index):
        return pl.ds(pl.multiple_of(index * group, 128), group)

    local_copies = [0]

    def local_copy(src, dst):
        k = local_copies[0]
        local_copies[0] += 1
        c = pltpu.make_async_copy(src, dst, load_sem.at[k])
        c.start()
        return c

    load_ctx = local_copy(ctx_hbm, C.at[x])
    load_grad = local_copy(grad_hbm, GI)
    load_down = local_copy(down_hbm, DIN)
    load_exp = local_copy(exp_hbm, EXP)
    load_codes = local_copy(codes_hbm, W.at[0:COLS])
    load_rest = [local_copy(map_hbm, MAP), local_copy(up_hbm, UP), local_copy(res_hbm, RES)]

    barrier = pltpu.get_barrier_semaphore()

    def greet(device):
        pl.semaphore_signal(barrier, inc=1, device_id=device, device_id_type=MESH)

    for r in range(1, NX):
        greet(dev_x(r))
    for r in range(1, NZ):
        greet(dev_z(r))
    for r in range(1, NY):
        greet(dev_y(r))
    greet(other_core)

    counter = [0]

    def copy(src, dst, device):
        k = counter[0]
        counter[0] += 1
        return pltpu.make_async_remote_copy(
            src_ref=src, dst_ref=dst, send_sem=send_sem.at[k], recv_sem=recv_sem.at[k],
            device_id=device, device_id_type=MESH,
        )

    pending = []

    def start(c):
        c.start()
        pending.append(c)
        return c

    def arrived(pair):
        for c in pair:
            c.wait_recv()

    load_down.wait()
    DX[x] = jnp.concatenate([DIN[...], jnp.zeros((RANK, 96), BF16)], axis=1)
    load_ctx.wait()

    pl.semaphore_wait(barrier, (NX - 1) + (NZ - 1) + (NY - 1) + 1)

    def z_ring(step, column, lo, mid, hi):
        if step < 4:
            right = copy(
                C.at[((NZ - step + 1) % NZ) * NX + column, lo:hi], C.at[(NZ - step) * NX + column, lo:hi], dev_z(1)
            )
            left = copy(C.at[(step - 1) * NX + column, lo:hi], C.at[step * NX + column, lo:hi], dev_z(NZ - 1))
        else:
            right = copy(C.at[5 * NX + column, lo:mid], C.at[4 * NX + column, lo:mid], dev_z(1))
            left = copy(C.at[3 * NX + column, mid:hi], C.at[4 * NX + column, mid:hi], dev_z(NZ - 1))
        return start(right), start(left)

    def qz(step):
        return z_ring(step, x, 0, 48, QR)

    def pz(step, column):
        return z_ring(step, column, QR, QR + PH, ROWS)

    def x_first(rz, lo, hi):
        own = C.at[rz * NX + x, lo:hi]
        return start(copy(own, own, dev_x(1))), start(copy(own, own, dev_x(NX - 1)))

    def x_second(rz, lo, mid, hi):
        a = C.at[rz * NX + before, lo:mid]
        b = C.at[rz * NX + after, mid:hi]
        return start(copy(a, a, dev_x(1))), start(copy(b, b, dev_x(NX - 1)))

    qz_c, qx1, qx2, pz_c = {}, {}, {}, {}

    def q_first(*places):
        for rz in places:
            qx1[rz] = x_first(rz, 0, QR)

    def q_second(*places):
        for rz in places:
            arrived(qx1[rz])
            qx2[rz] = x_second(rz, 0, 48, QR)

    def p_next(step, column, name):
        if step > 1:
            arrived(pz_c[name, step - 1])
        pz_c[name, step] = pz(step, column)

    def dn_ring(step):
        if step < 4:
            right = copy(DN.at[(NZ - step + 1) % NZ], DN.at[NZ - step], dev_z(1))
            left = copy(DN.at[step - 1], DN.at[step], dev_z(NZ - 1))
            return start(right), start(left)
        return (start(copy(DN.at[5], DN.at[4], dev_z(1))),)

    qz_c[1] = qz(1)
    px1 = x_first(0, QR, ROWS)
    dx = [start(copy(DX.at[x], DX.at[x], dev_x(r))) for r in range(1, NX)]
    p_next(1, x, "own")
    q_first(0)

    load_exp.wait()
    codes_scale = EXP[...]
    factor = jnp.where(
        codes_scale == -3, 0.125,
        jnp.where(codes_scale == -2, 0.25, jnp.where(codes_scale == -1, 0.5, jnp.where(codes_scale == 0, 1.0, 2.0))),
    ).astype(F32)
    for j in range(COLS // BLKC):
        GS[j * BLKC : (j + 1) * BLKC, :] = jnp.broadcast_to(factor[j : j + 1, :], (BLKC, DIMS // BLKR))
    load_codes.wait()

    picked = (
        lax.broadcasted_iota(jnp.int32, (DIMS // BLKR, 128), 0)
        == y * (group // BLKR) + lax.broadcasted_iota(jnp.int32, (DIMS // BLKR, 128), 1)
    )
    slab_scale = dot(GS[...].astype(BF16), picked.astype(F32).astype(BF16))
    for i in range(group // BLKR):
        lanes = pl.ds(pl.multiple_of(y * group + i * BLKR, BLKR), BLKR)
        SLAB[:, i * BLKR : (i + 1) * BLKR] = (W[0:COLS, lanes].astype(F32) * slab_scale[:, i : i + 1]).astype(BF16)
    WS[...] = SLAB[...].T.reshape(NX, 2, ROWS // 2, COLS)
    wx = []
    for r in range(1, NX):
        wx.append(start(copy(WS.at[lax.rem(x + r, NX), core], WX.at[NX - r, y, core], dev_x(r))))

    load_grad.wait()
    for i in range(32):
        g = GI[:, i * COLS : (i + 1) * COLS].astype(F32)
        last = [g[4 * q : 4 * q + 4, 256:COLS] for q in range(3)]
        side = jnp.concatenate(last + [jnp.zeros((4, 64), F32)], axis=1)
        GM[i % NX, i // NX] = jnp.concatenate([g[:, 0:256], side], axis=0).astype(BF16)
    gx = [start(copy(GM.at[lax.rem(x + r, NX)], A1.at[x], dev_x(r))) for r in range(1, NX)]
    A1[x] = GM[x]

    arrived(qz_c[1])
    qz_c[2] = qz(2)
    q_first(1, 7)
    arrived(px1)
    px2 = x_second(0, QR, QR + PH, ROWS)
    p_next(1, before, "before")
    p_next(1, after, "after")
    p_next(2, x, "own")
    def y_unit(rel):
        return WX.at[1:NX, lax.rem(y + rel, NY), core]

    y_c = {}

    def y_ring(step):
        for r in range(1, NX):
            if step > 1:
                arrived(y_c[r, step - 1])
            if step < 4:
                a = WX.at[r, lax.rem(y + NY - step + 1, NY), core]
                b = WX.at[r, lax.rem(y + step - 1, NY), core]
            else:
                a = WX.at[r, lax.rem(y + 5, NY), core, 0:48]
                b = WX.at[r, lax.rem(y + 3, NY), core, 48:80]
            y_c[r, step] = (start(copy(a, a, dev_y(1))), start(copy(b, b, dev_y(NY - 1))))

    swaps = []

    def core_swap(*places):
        for rel in places:
            a = y_unit(rel)
            swaps.append(start(copy(a, a, other_core)))

    for c in wx:
        c.wait_recv()
    y_ring(1)
    core_swap(0)
    for c in dx:
        c.wait_recv()
    DN[0] = jnp.concatenate([DX[i, :, 0:ROWS] for i in range(NX)], axis=1)
    dn1 = dn_ring(1)
    for c in gx:
        c.wait_recv()
    A2[z] = A1[:, z]
    gz = [start(copy(A1.at[:, lax.rem(z + r, NZ)], A2.at[z], dev_z(r))) for r in range(1, NZ)]

    for b in range(DIMS // BLKR):
        lanes = slice(b * BLKR, (b + 1) * BLKR)
        W[0:COLS, lanes] = (W[0:COLS, lanes].astype(F32) * GS[:, b : b + 1]).astype(BF16)

    q_second(0)
    arrived(qz_c[2])
    qz_c[3] = qz(3)
    q_first(2, 6)
    arrived(px2)
    p_next(1, opposite, "opposite")
    for c in gz:
        c.wait_recv()
    away = (1 - sec) * (NZ // 2)
    am = (
        start(copy(A2.at[pl.ds(away, 2)], AM.at[0], dev_y(2))),
        start(copy(A2.at[pl.ds(away + 2, 2)], AM.at[1], dev_y(NY - 2))),
    )

    q_second(1, 7)
    p_next(2, before, "before")
    p_next(2, after, "after")
    p_next(3, x, "own")
    arrived(dn1)
    dn2 = dn_ring(2)
    y_ring(2)
    core_swap(1, 7)
    arrived(am)
    ga = (start(copy(AM.at[0], A3.at[0:2], dev_y(2))), start(copy(AM.at[1], A3.at[2:4], dev_y(NY - 2))))

    def turn(k):
        WT[...] = W[0:COLS, pl.ds(pl.multiple_of(k * group + x * BLKR, BLKR), 256)].T
        rows = WT[pl.ds(pl.multiple_of(x * 32, 32), ROWS), :]
        WX[0, k] = rows.reshape(2, ROWS // 2, COLS)


    arrived(qz_c[3])
    qz_c[4] = qz(4)
    q_first(3, 5)
    p_next(2, opposite, "opposite")
    q_second(2, 6)
    p_next(3, before, "before")
    p_next(3, after, "after")
    p_next(4, x, "own")
    arrived(dn2)
    dn3 = dn_ring(3)
    y_ring(3)
    core_swap(2, 6)
    for k in range(NZ // 2):
        turn(k)

    arrived(qz_c[4])
    q_first(4)
    p_next(3, opposite, "opposite")
    q_second(3, 5)
    p_next(4, before, "before")
    p_next(4, after, "after")
    arrived(dn3)
    dn4 = dn_ring(4)
    y_ring(4)
    core_swap(3, 5)
    for k in range(NZ // 2, NZ):
        turn(k)

    ACC[...] = jnp.zeros_like(ACC)

    def forward(rz):
        if rz == 4:
            for name in ("own", "before", "after", "opposite"):
                arrived(pz_c[name, 4])
        arrived(qx2[rz])
        lanes = w_lanes(lax.rem(z + rz, NZ))
        W[COLS : COLS + RANK, lanes] = DN[rz]
        ACC[...] += dot(W[:, lanes], C[rz * NX : (rz + 1) * NX].reshape(group, CROP))

    q_second(4)
    p_next(4, opposite, "opposite")
    forward(0)
    forward(1)
    forward(7)

    for c in load_rest:
        c.wait()
    arrived(ga)
    residue = MAP[...]
    block = lax.shift_right_logical(residue * 43691, 19)
    row = residue - block * OWNED
    quarter = lax.shift_right_logical(row, 2)
    token = lax.broadcasted_iota(jnp.int32, (1, CROP), 1)
    valid = token < len_ref[0]
    parity = block & 1
    slot = lax.shift_right_logical(block, 1) + jnp.where(parity == sec, 0, 16)
    place = jnp.where(valid, slot * SLOT + row, -1)
    place_last = jnp.where(valid, slot * SLOT + OWNED + (row - quarter * 4), -1)
    index = lax.broadcasted_iota(jnp.int32, (32 * SLOT, CROP), 0)
    mine = A2[pl.ds(sec * (NZ // 2), NZ // 2)].reshape(16 * SLOT, 256)
    rows = jnp.concatenate([mine, A3[...].reshape(16 * SLOT, 256)], axis=0)
    most = dot(rows, (index == place).astype(F32).astype(BF16), ((0,), (0,)))
    last = dot(rows, (index == place_last).astype(F32).astype(BF16), ((0,), (0,)))
    last = jnp.where(quarter == 0, last[0:64], jnp.where(quarter == 1, last[64:128], last[128:192]))
    upstream = jnp.concatenate([most, last], axis=0)
    gain = jnp.broadcast_to(gain_ref[...].astype(F32).reshape(1, COLS), (8, COLS)).T[:, 0:1]
    scaled = gain * upstream

    forward(2)
    forward(6)
    forward(3)
    forward(5)
    arrived(dn4)
    forward(4)

    inner = ACC[COLS : COLS + RANK, :].astype(BF16)
    hidden = ACC[0:COLS, :] + ADAPTER_SCALE * dot(UP[...], inner, ((0,), (0,))) + RES[...].astype(F32)
    ST[0:1, :] = jnp.sum(hidden, axis=0, keepdims=True)
    ST[1:2, :] = jnp.sum(hidden * hidden, axis=0, keepdims=True)
    ST[2:3, :] = jnp.sum(scaled, axis=0, keepdims=True)
    ST[3:4, :] = jnp.sum(scaled * hidden, axis=0, keepdims=True)
    sx = [start(copy(ST, SX.at[r], dev_x(r))) for r in range(1, NX)]
    for c in sx:
        c.wait_recv()
    SZ[0] = (ST[...] + SX[1]) + (SX[2] + SX[3])
    sz = [start(copy(SZ.at[0], SZ.at[r], dev_z(r))) for r in range(1, NZ)]
    for r in range(1, NX):
        arrived(y_c[r, 4])
    core_swap(4)
    for c in sz:
        c.wait_recv()
    sums = jnp.sum(SZ[...], axis=0) / MODEL_WIDTH
    average = sums[0:1, :]
    variance = sums[1:2, :] - average * average
    inverse = lax.rsqrt(variance + 1e-05)
    first_mean = sums[2:3, :]
    second_mean = inverse * (sums[3:4, :] - average * first_mean)
    normed = (hidden - average) * inverse
    gradient = (inverse * (scaled - first_mean - normed * second_mean)).astype(BF16)
    for b in range(NBLOCK):
        HX[b, 0] = gradient[:, b * TOKEN_BLOCK : (b + 1) * TOKEN_BLOCK]

    def hx_first(b):
        return (
            start(copy(HX.at[b, 0], HX.at[b, 3], dev_x(1))),
            start(copy(HX.at[b, 0], HX.at[b, 1], dev_x(NX - 1))),
        )

    def hx_second(b):
        arrived(h1[b])
        return (
            start(copy(HX.at[b, 3, 0:160], HX.at[b, 2, 0:160], dev_x(1))),
            start(copy(HX.at[b, 1, 160:COLS], HX.at[b, 2, 160:COLS], dev_x(NX - 1))),
        )

    h1 = [hx_first(0), hx_first(1)]
    TX[0] = dot(UP[...], gradient).astype(BF16)
    tx = [start(copy(TX.at[0], TX.at[r], dev_x(r))) for r in range(1, NX)]
    UA[...] = ADAPTER_SCALE * dot(inner, gradient, ((1,), (1,)))
    uc = start(copy(UA, UC, other_core))
    HG[...] = gradient
    out_hg = local_copy(HG, hg_out)
    FH[...] = (gain * normed).astype(BF16)
    out_fh = local_copy(FH, fh_out)
    h2 = [hx_second(0)]
    h1.append(hx_first(2))
    for c in tx:
        c.wait_recv()
    TZ[0] = jnp.sum(TX[...].astype(F32), axis=0).astype(BF16)
    tz = [start(copy(TZ.at[0], TZ.at[r], dev_z(r))) for r in range(1, NZ)]
    uc.wait_recv()
    UY[0] = UA[...] + UC[...]
    uy = [start(copy(UY.at[0], UY.at[r], dev_y(r))) for r in range(1, NY)]
    h2.append(hx_second(1))
    for c in swaps:
        c.wait_recv()

    halves = NZ * ROWS // 2

    def partials(b):
        arrived(h2[b])

        @pl.loop(0, 2)
        def _(h):
            total = jnp.zeros((halves, TOKEN_BLOCK), F32)
            for r in range(NX):
                w = WX[r, pl.ds(h * (NZ // 2), NZ // 2)].reshape(halves, COLS)
                total = total + dot(w, HX[b, r])
            PART[b, pl.ds(h * (NZ // 2), NZ // 2)] = total.reshape(NZ // 2, ROWS, TOKEN_BLOCK)

    def part(b, rel):
        return PART[b, lax.rem(z + rel, NZ)]

    HALF = ROWS // 2
    rs = {}

    def rs_step(b, step):
        if step == 1:
            for side, three in ((0, 3), (1, 5)):
                lo, hi = (0, HALF) if side == 0 else (HALF, ROWS)
                RS[b, side, 0, 0:HALF] = part(b, 4)[lo:hi].astype(BF16)
                RS[b, side, 1] = part(b, three).astype(BF16)
            rs[b, 1] = (
                start(copy(RS.at[b, 0, 0, 0:HALF], RR.at[b, 0, 0:HALF], dev_z(2))),
                start(copy(RS.at[b, 1, 0, 0:HALF], LR.at[b, 0, 0:HALF], dev_z(NZ - 2))),
                start(copy(RS.at[b, 0, 1], RR.at[b, 1], dev_z(1))),
                start(copy(RS.at[b, 1, 1], LR.at[b, 1], dev_z(NZ - 1))),
            )
            RS[b, 0, 2] = part(b, 1).astype(BF16)
            RS[b, 1, 2] = part(b, 7).astype(BF16)
            rs[b, 4] = (
                start(copy(RS.at[b, 0, 2], RR.at[b, 2], dev_z(1))),
                start(copy(RS.at[b, 1, 2], LR.at[b, 2], dev_z(NZ - 1))),
            )
        else:
            arrived(rs[b, 1])
            right = part(b, 2) + RR[b, 1].astype(F32)
            left = part(b, 6) + LR[b, 1].astype(F32)
            RS[b, 0, 3, 0:HALF] = (right[0:HALF] + RR[b, 0, 0:HALF].astype(F32)).astype(BF16)
            RS[b, 0, 3, HALF:ROWS] = right[HALF:ROWS].astype(BF16)
            RS[b, 1, 3, 0:HALF] = left[0:HALF].astype(BF16)
            RS[b, 1, 3, HALF:ROWS] = (left[HALF:ROWS] + LR[b, 0, 0:HALF].astype(F32)).astype(BF16)
            rs[b, 4] += (
                start(copy(RS.at[b, 0, 3], RR.at[b, 3], dev_z(2))),
                start(copy(RS.at[b, 1, 3], LR.at[b, 3], dev_z(NZ - 2))),
            )

    partials(0)
    rs_step(0, 1)
    h2.append(hx_second(2))
    partials(1)
    rs_step(1, 1)
    for c in tz:
        c.wait_recv()
    through_all = jnp.sum(TZ[...].astype(F32), axis=0).astype(BF16)
    DA[...] = ADAPTER_SCALE * dot(through_all, C[x], ((1,), (1,)))
    dc = start(copy(DA, DC, other_core))
    rs_step(0, 2)
    partials(2)
    rs_step(2, 1)
    dc.wait_recv()
    DY[0] = DA[...] + DC[...]
    dy = [start(copy(DY.at[0], DY.at[r], dev_y(r))) for r in range(1, NY)]
    adapter = ADAPTER_SCALE * dot(DIN[...], through_all, ((0,), (0,)))
    rs_step(1, 2)
    rs_step(2, 2)
    for c in uy:
        c.wait_recv()
    UG[...] = jnp.sum(UY[...], axis=0)
    out_ug = local_copy(UG, ug_out)
    for c in dy:
        c.wait_recv()
    DG[...] = jnp.sum(DY[...], axis=0)
    out_dg = local_copy(DG, dg_out)
    for b in range(NBLOCK):
        arrived(rs[b, 4])
        lanes = slice(b * TOKEN_BLOCK, (b + 1) * TOKEN_BLOCK)
        total = part(b, 0) + (RR[b, 2].astype(F32) + LR[b, 2].astype(F32))
        total = total + (RR[b, 3].astype(F32) + LR[b, 3].astype(F32))
        CG[:, lanes] = (total + adapter[:, lanes]).astype(BF16)
    out_cg = local_copy(CG, cg_out)

    for c in pending:
        c.wait_send()

    for c in (out_hg, out_fh, out_ug, out_dg, out_cg):
        c.wait()


def finish(*refs):
    arrays, outs, held, sems = refs[:5], refs[5:10], refs[10:15], refs[15]
    loads = [pltpu.make_async_copy(a, h, sems.at[0, i]) for i, (a, h) in enumerate(zip(arrays, held))]
    stores = [pltpu.make_async_copy(h, o, sems.at[1, i]) for i, (h, o) in enumerate(zip(held, outs))]
    for c in loads:
        c.start()
    for load, store in zip(loads, stores):
        load.wait()
        store.start()
    for c in stores:
        c.wait()


def on_device(grad, context, residual, gain, codes, exponents, down, up, residue_map, lengths):
    vmem = pl.BlockSpec(memory_space=pltpu.VMEM)
    anywhere = pl.BlockSpec(memory_space=pl.ANY)
    shapes = (
        jax.ShapeDtypeStruct((ROWS, CROP), BF16),
        jax.ShapeDtypeStruct((COLS, CROP), BF16),
        jax.ShapeDtypeStruct((RANK, ROWS), F32),
        jax.ShapeDtypeStruct((RANK, COLS), F32),
        jax.ShapeDtypeStruct((COLS, CROP), BF16),
    )
    results = pl.pallas_call(
        kernel,
        out_shape=shapes,
        in_specs=[anywhere] * 3 + [vmem] + [anywhere] * 5 + [pl.BlockSpec(memory_space=pltpu.SMEM)],
        out_specs=[anywhere] * 5,
        scratch_shapes=[
            pltpu.VMEM((COLS + RANK, DIMS), BF16),
            pltpu.VMEM((NX * NZ, ROWS, CROP), BF16),
            pltpu.VMEM((NX, RANK, 256), BF16),
            pltpu.VMEM((NZ, RANK, NX * ROWS), BF16),
            pltpu.VMEM((COLS, NX * ROWS), BF16),
            pltpu.VMEM((NX, 2, ROWS // 2, COLS), BF16),
            pltpu.VMEM((256, COLS), BF16),
            pltpu.VMEM((NX, NZ, 2, ROWS // 2, COLS), BF16),
            pltpu.VMEM((OWNED, MODEL_WIDTH), BF16),
            pltpu.VMEM((NX, NZ, SLOT, 256), BF16),
            pltpu.VMEM((NX, NZ, SLOT, 256), BF16),
            pltpu.VMEM((NZ, NX, SLOT, 256), BF16),
            pltpu.VMEM((2, 2, NX, SLOT, 256), BF16),
            pltpu.VMEM((NZ // 2, NX, SLOT, 256), BF16),
            pltpu.VMEM((COLS + RANK, CROP), F32),
            pltpu.VMEM((NBLOCK, NX, COLS, TOKEN_BLOCK), BF16),
            pltpu.VMEM((NBLOCK, NZ, ROWS, TOKEN_BLOCK), F32),
            pltpu.VMEM((NBLOCK, 2, 4, ROWS, TOKEN_BLOCK), BF16),
            pltpu.VMEM((NBLOCK, 4, ROWS, TOKEN_BLOCK), BF16),
            pltpu.VMEM((NBLOCK, 4, ROWS, TOKEN_BLOCK), BF16),
            pltpu.VMEM((4, CROP), F32),
            pltpu.VMEM((NX, 4, CROP), F32),
            pltpu.VMEM((NZ, 4, CROP), F32),
            pltpu.VMEM((NX, RANK, CROP), BF16),
            pltpu.VMEM((NZ, RANK, CROP), BF16),
            pltpu.VMEM((RANK, COLS), F32),
            pltpu.VMEM((RANK, COLS), F32),
            pltpu.VMEM((NY, RANK, COLS), F32),
            pltpu.VMEM((RANK, ROWS), F32),
            pltpu.VMEM((RANK, ROWS), F32),
            pltpu.VMEM((NY, RANK, ROWS), F32),
            pltpu.VMEM((COLS, DIMS // BLKR), F32),
            pltpu.VMEM((COLS, CROP), BF16),
            pltpu.VMEM((COLS // BLKC, DIMS // BLKR), jnp.int32),
            pltpu.VMEM((RANK, ROWS), BF16),
            pltpu.VMEM((RANK, COLS), BF16),
            pltpu.VMEM((1, CROP), jnp.int32),
            pltpu.VMEM((ROWS, CROP), BF16),
            pltpu.VMEM((COLS, CROP), BF16),
            pltpu.VMEM((RANK, ROWS), F32),
            pltpu.VMEM((RANK, COLS), F32),
            pltpu.VMEM((COLS, CROP), BF16),
            pltpu.SemaphoreType.DMA((SENDS,)),
            pltpu.SemaphoreType.DMA((SENDS,)),
            pltpu.SemaphoreType.DMA((16,)),
        ],
        compiler_params=pltpu.CompilerParams(
            collective_id=0, has_side_effects=True, vmem_limit_bytes=56 * 1024 * 1024
        ),
        cost_estimate=pl.CostEstimate(flops=2 * 2 * CROP * DIMS * COLS, bytes_accessed=8 << 20, transcendentals=0),
    )(grad, context.T, residual.T, gain, codes.T, exponents.T, down.T, up, residue_map, lengths)
    cg, hg, dg, ug, fh = pl.pallas_call(
        finish,
        out_shape=shapes,
        in_specs=[anywhere] * 5,
        out_specs=[anywhere] * 5,
        scratch_shapes=[pltpu.VMEM(a.shape, a.dtype) for a in shapes] + [pltpu.SemaphoreType.DMA((2, 5))],
    )(*results)
    return cg, hg.T, dg.T, ug, fh.T


def solution(mesh):
    in_specs = (
        P(("dp", "tensor", "section"), None),
        P(("dp", "section"), "tensor"),
        P(("dp", "section"), "tensor"),
        P("tensor"),
        P(None, "tensor"),
        P(None, "tensor"),
        P("tensor", None),
        P(None, "tensor"),
        P(("dp", "section"), None),
        P(("dp", "section")),
    )
    out_specs = (
        P("tensor", ("dp", "section")),
        P(("dp", "section"), "tensor"),
        P("tensor", None),
        P(None, "tensor"),
        P(("dp", "section"), "tensor"),
    )
    return jax.shard_map(
        on_device, mesh=mesh, in_specs=in_specs, out_specs=out_specs, check_vma=False
    )
```

```python
import functools

import jax
import jax.numpy as jnp
from jax import lax
from jax.experimental import pallas as pl
from jax.experimental.pallas import tpu as pltpu
from jax.sharding import PartitionSpec as P

MODEL_WIDTH = 10240
DIMS = 5120
ADAPTER_SCALE = 2.0
CROP = 384
COLS = 320
ROWS = 160
RANK = 16
NX = 4
NZ = 8
NY = 8
BLKR = 128
BLKC = 64
OWNED = 12
SLOT = 16
F32 = jnp.float32
BF16 = jnp.bfloat16
MESH = pl.DeviceIdType.MESH
QR = 96
PH = 32
TOKEN_BLOCK = 128
NBLOCK = CROP // TOKEN_BLOCK

SENDS = 256


def dot(a, b, dims=((1,), (0,))):
    return lax.dot_general(a, b, (dims, ((), ())), preferred_element_type=F32)


def kernel(
    grad_hbm, ctx_hbm, res_hbm, gain_ref, codes_hbm, exp_hbm, down_hbm, up_hbm, map_hbm, len_ref,
    cg_out, hg_out, dg_out, ug_out, fh_out,
    W, C, DX, DN, SLAB, WS, WT, WX, GI, GM, A1, A2, AM, A3, ACC, HX, PART, RS, RR, LR, ST, SX, SZ, TX, TZ,
    UA, UC, UY, DA, DC, DY, GS, RES, EXP, DIN, UP, MAP, CG, HG, DG, UG, FH,
    send_sem, recv_sem, load_sem,
):
    dp = lax.axis_index("dp")
    t = lax.axis_index("tensor")
    sec = lax.axis_index("section")
    x = lax.rem(t, NX)
    z = lax.div(t, NX)
    core = lax.rem(dp, 2)
    y = sec * (NY // 2) + lax.div(dp, 2)

    def dev_x(r):
        return (dp, z * NX + lax.rem(x + r, NX), sec)

    def dev_z(r):
        return (dp, lax.rem(z + r, NZ) * NX + x, sec)

    def dev_y(r):
        other = lax.rem(y + r, NY)
        return (lax.rem(other, NY // 2) * 2 + core, t, lax.div(other, NY // 2))

    other_core = (dp + 1 - 2 * core, t, sec)
    before, after, opposite = lax.rem(x + 3, NX), lax.rem(x + 1, NX), lax.rem(x + 2, NX)

    group = NX * ROWS

    def w_lanes(index):
        return pl.ds(pl.multiple_of(index * group, 128), group)

    local_copies = [0]

    def local_copy(src, dst):
        k = local_copies[0]
        local_copies[0] += 1
        c = pltpu.make_async_copy(src, dst, load_sem.at[k])
        c.start()
        return c

    load_ctx = local_copy(ctx_hbm, C.at[x])
    load_grad = local_copy(grad_hbm, GI)
    load_down = local_copy(down_hbm, DIN)
    load_exp = local_copy(exp_hbm, EXP)
    load_codes = local_copy(codes_hbm, W.at[0:COLS])
    load_rest = [local_copy(map_hbm, MAP), local_copy(up_hbm, UP), local_copy(res_hbm, RES)]

    barrier = pltpu.get_barrier_semaphore()

    def greet(device):
        pl.semaphore_signal(barrier, inc=1, device_id=device, device_id_type=MESH)

    for r in range(1, NX):
        greet(dev_x(r))
    for r in range(1, NZ):
        greet(dev_z(r))
    for r in range(1, NY):
        greet(dev_y(r))
    greet(other_core)

    counter = [0]

    def copy(src, dst, device):
        k = counter[0]
        counter[0] += 1
        return pltpu.make_async_remote_copy(
            src_ref=src, dst_ref=dst, send_sem=send_sem.at[k], recv_sem=recv_sem.at[k],
            device_id=device, device_id_type=MESH,
        )

    pending = []

    def start(c):
        c.start()
        pending.append(c)
        return c

    def arrived(pair):
        for c in pair:
            c.wait_recv()

    def drain(count):
        for c in pending[:count]:
            c.wait_send()
        del pending[:count]

    load_down.wait()
    DX[x] = jnp.concatenate([DIN[...], jnp.zeros((RANK, 96), BF16)], axis=1)
    load_ctx.wait()

    pl.semaphore_wait(barrier, (NX - 1) + (NZ - 1) + (NY - 1) + 1)

    def z_ring(step, column, lo, mid, hi):
        if step < 4:
            right = copy(
                C.at[((NZ - step + 1) % NZ) * NX + column, lo:hi], C.at[(NZ - step) * NX + column, lo:hi], dev_z(1)
            )
            left = copy(C.at[(step - 1) * NX + column, lo:hi], C.at[step * NX + column, lo:hi], dev_z(NZ - 1))
        else:
            right = copy(C.at[5 * NX + column, lo:mid], C.at[4 * NX + column, lo:mid], dev_z(1))
            left = copy(C.at[3 * NX + column, mid:hi], C.at[4 * NX + column, mid:hi], dev_z(NZ - 1))
        return start(right), start(left)

    def qz(step):
        return z_ring(step, x, 0, 48, QR)

    def pz(step, column):
        return z_ring(step, column, QR, QR + PH, ROWS)

    def x_first(rz, lo, hi):
        own = C.at[rz * NX + x, lo:hi]
        return start(copy(own, own, dev_x(1))), start(copy(own, own, dev_x(NX - 1)))

    def x_second(rz, lo, mid, hi):
        a = C.at[rz * NX + before, lo:mid]
        b = C.at[rz * NX + after, mid:hi]
        return start(copy(a, a, dev_x(1))), start(copy(b, b, dev_x(NX - 1)))

    qz_c, qx1, qx2, pz_c = {}, {}, {}, {}

    def q_first(*places):
        for rz in places:
            qx1[rz] = x_first(rz, 0, QR)

    def q_second(*places):
        for rz in places:
            arrived(qx1[rz])
            qx2[rz] = x_second(rz, 0, 48, QR)

    def p_next(step, column, name):
        if step > 1:
            arrived(pz_c[name, step - 1])
        pz_c[name, step] = pz(step, column)

    def dn_ring(step):
        if step < 4:
            right = copy(DN.at[(NZ - step + 1) % NZ], DN.at[NZ - step], dev_z(1))
            left = copy(DN.at[step - 1], DN.at[step], dev_z(NZ - 1))
            return start(right), start(left)
        return (start(copy(DN.at[5], DN.at[4], dev_z(1))),)

    qz_c[1] = qz(1)
    px1 = x_first(0, QR, ROWS)
    dx = [start(copy(DX.at[x], DX.at[x], dev_x(r))) for r in range(1, NX)]
    p_next(1, x, "own")
    q_first(0)

    load_exp.wait()
    codes_scale = EXP[...]
    factor = jnp.where(
        codes_scale == -3, 0.125,
        jnp.where(codes_scale == -2, 0.25, jnp.where(codes_scale == -1, 0.5, jnp.where(codes_scale == 0, 1.0, 2.0))),
    ).astype(F32)
    for j in range(COLS // BLKC):
        GS[j * BLKC : (j + 1) * BLKC, :] = jnp.broadcast_to(factor[j : j + 1, :], (BLKC, DIMS // BLKR))
    load_codes.wait()

    picked = (
        lax.broadcasted_iota(jnp.int32, (DIMS // BLKR, 128), 0)
        == y * (group // BLKR) + lax.broadcasted_iota(jnp.int32, (DIMS // BLKR, 128), 1)
    )
    slab_scale = dot(GS[...].astype(BF16), picked.astype(F32).astype(BF16))
    for i in range(group // BLKR):
        lanes = pl.ds(pl.multiple_of(y * group + i * BLKR, BLKR), BLKR)
        SLAB[:, i * BLKR : (i + 1) * BLKR] = (W[0:COLS, lanes].astype(F32) * slab_scale[:, i : i + 1]).astype(BF16)
    WS[...] = SLAB[...].T.reshape(NX, 2, ROWS // 2, COLS)
    wx = []
    for r in range(1, NX):
        wx.append(start(copy(WS.at[lax.rem(x + r, NX), core], WX.at[NX - r, y, core], dev_x(r))))

    load_grad.wait()
    for i in range(32):
        g = GI[:, i * COLS : (i + 1) * COLS].astype(F32)
        last = [g[4 * q : 4 * q + 4, 256:COLS] for q in range(3)]
        side = jnp.concatenate(last + [jnp.zeros((4, 64), F32)], axis=1)
        GM[i % NX, i // NX] = jnp.concatenate([g[:, 0:256], side], axis=0).astype(BF16)
    gx = [start(copy(GM.at[lax.rem(x + r, NX)], A1.at[x], dev_x(r))) for r in range(1, NX)]
    A1[x] = GM[x]

    arrived(qz_c[1])
    qz_c[2] = qz(2)
    q_first(1, 7)
    arrived(px1)
    px2 = x_second(0, QR, QR + PH, ROWS)
    p_next(1, before, "before")
    p_next(1, after, "after")
    p_next(2, x, "own")
    def y_unit(rel):
        return WX.at[1:NX, lax.rem(y + rel, NY), core]

    y_c = {}

    def y_ring(step):
        for r in range(1, NX):
            if step > 1:
                arrived(y_c[r, step - 1])
            if step < 4:
                a = WX.at[r, lax.rem(y + NY - step + 1, NY), core]
                b = WX.at[r, lax.rem(y + step - 1, NY), core]
            else:
                a = WX.at[r, lax.rem(y + 5, NY), core, 0:48]
                b = WX.at[r, lax.rem(y + 3, NY), core, 48:80]
            y_c[r, step] = (start(copy(a, a, dev_y(1))), start(copy(b, b, dev_y(NY - 1))))

    swaps = []

    def core_swap(*places):
        for rel in places:
            a = y_unit(rel)
            swaps.append(start(copy(a, a, other_core)))

    for c in wx:
        c.wait_recv()
    y_ring(1)
    core_swap(0)
    for c in dx:
        c.wait_recv()
    DN[0] = jnp.concatenate([DX[i, :, 0:ROWS] for i in range(NX)], axis=1)
    dn1 = dn_ring(1)
    for c in gx:
        c.wait_recv()
    A2[z] = A1[:, z]
    gz = [start(copy(A1.at[:, lax.rem(z + r, NZ)], A2.at[z], dev_z(r))) for r in range(1, NZ)]

    for b in range(DIMS // BLKR):
        lanes = slice(b * BLKR, (b + 1) * BLKR)
        W[0:COLS, lanes] = (W[0:COLS, lanes].astype(F32) * GS[:, b : b + 1]).astype(BF16)

    q_second(0)
    arrived(qz_c[2])
    qz_c[3] = qz(3)
    q_first(2, 6)
    arrived(px2)
    p_next(1, opposite, "opposite")
    for c in gz:
        c.wait_recv()
    away = (1 - sec) * (NZ // 2)
    am = (
        start(copy(A2.at[pl.ds(away, 2)], AM.at[0], dev_y(2))),
        start(copy(A2.at[pl.ds(away + 2, 2)], AM.at[1], dev_y(NY - 2))),
    )

    q_second(1, 7)
    p_next(2, before, "before")
    p_next(2, after, "after")
    p_next(3, x, "own")
    arrived(dn1)
    dn2 = dn_ring(2)
    y_ring(2)
    core_swap(1, 7)
    arrived(am)
    ga = (start(copy(AM.at[0], A3.at[0:2], dev_y(2))), start(copy(AM.at[1], A3.at[2:4], dev_y(NY - 2))))

    def turn(k):
        WT[...] = W[0:COLS, pl.ds(pl.multiple_of(k * group + x * BLKR, BLKR), 256)].T
        rows = WT[pl.ds(pl.multiple_of(x * 32, 32), ROWS), :]
        WX[0, k] = rows.reshape(2, ROWS // 2, COLS)


    arrived(qz_c[3])
    qz_c[4] = qz(4)
    q_first(3, 5)
    p_next(2, opposite, "opposite")
    q_second(2, 6)
    p_next(3, before, "before")
    p_next(3, after, "after")
    p_next(4, x, "own")
    arrived(dn2)
    dn3 = dn_ring(3)
    y_ring(3)
    core_swap(2, 6)
    for k in range(NZ // 2):
        turn(k)

    early = len(pending)
    arrived(qz_c[4])
    q_first(4)
    p_next(3, opposite, "opposite")
    q_second(3, 5)
    p_next(4, before, "before")
    p_next(4, after, "after")
    arrived(dn3)
    dn4 = dn_ring(4)
    y_ring(4)
    core_swap(3, 5)
    for k in range(NZ // 2, NZ):
        turn(k)

    ACC[...] = jnp.zeros_like(ACC)

    def forward(rz):
        if rz == 4:
            for name in ("own", "before", "after", "opposite"):
                arrived(pz_c[name, 4])
        arrived(qx2[rz])
        lanes = w_lanes(lax.rem(z + rz, NZ))
        W[COLS : COLS + RANK, lanes] = DN[rz]
        ACC[...] += dot(W[:, lanes], C[rz * NX : (rz + 1) * NX].reshape(group, CROP))

    q_second(4)
    p_next(4, opposite, "opposite")
    forward(0)
    forward(1)
    forward(7)

    for c in load_rest:
        c.wait()
    arrived(ga)
    residue = MAP[...]
    block = lax.shift_right_logical(residue * 43691, 19)
    row = residue - block * OWNED
    quarter = lax.shift_right_logical(row, 2)
    token = lax.broadcasted_iota(jnp.int32, (1, CROP), 1)
    valid = token < len_ref[0]
    parity = block & 1
    slot = lax.shift_right_logical(block, 1) + jnp.where(parity == sec, 0, 16)
    place = jnp.where(valid, slot * SLOT + row, -1)
    place_last = jnp.where(valid, slot * SLOT + OWNED + (row - quarter * 4), -1)
    index = lax.broadcasted_iota(jnp.int32, (32 * SLOT, CROP), 0)
    mine = A2[pl.ds(sec * (NZ // 2), NZ // 2)].reshape(16 * SLOT, 256)
    rows = jnp.concatenate([mine, A3[...].reshape(16 * SLOT, 256)], axis=0)
    most = dot(rows, (index == place).astype(F32).astype(BF16), ((0,), (0,)))
    last = dot(rows, (index == place_last).astype(F32).astype(BF16), ((0,), (0,)))
    last = jnp.where(quarter == 0, last[0:64], jnp.where(quarter == 1, last[64:128], last[128:192]))
    upstream = jnp.concatenate([most, last], axis=0)
    gain = jnp.broadcast_to(gain_ref[...].astype(F32).reshape(1, COLS), (8, COLS)).T[:, 0:1]
    scaled = gain * upstream

    forward(2)
    forward(6)
    forward(3)
    forward(5)
    arrived(dn4)
    forward(4)

    gathered = len(pending) - early
    inner = ACC[COLS : COLS + RANK, :].astype(BF16)
    hidden = ACC[0:COLS, :] + ADAPTER_SCALE * dot(UP[...], inner, ((0,), (0,))) + RES[...].astype(F32)
    ST[0:1, :] = jnp.sum(hidden, axis=0, keepdims=True)
    ST[1:2, :] = jnp.sum(hidden * hidden, axis=0, keepdims=True)
    ST[2:3, :] = jnp.sum(scaled, axis=0, keepdims=True)
    ST[3:4, :] = jnp.sum(scaled * hidden, axis=0, keepdims=True)
    sx = [start(copy(ST, SX.at[r], dev_x(r))) for r in range(1, NX)]
    for c in sx:
        c.wait_recv()
    SZ[0] = (ST[...] + SX[1]) + (SX[2] + SX[3])
    sz = [start(copy(SZ.at[0], SZ.at[r], dev_z(r))) for r in range(1, NZ)]
    for r in range(1, NX):
        arrived(y_c[r, 4])
    core_swap(4)
    drain(early)
    for c in sz:
        c.wait_recv()
    sums = jnp.sum(SZ[...], axis=0) / MODEL_WIDTH
    average = sums[0:1, :]
    variance = sums[1:2, :] - average * average
    inverse = lax.rsqrt(variance + 1e-05)
    first_mean = sums[2:3, :]
    second_mean = inverse * (sums[3:4, :] - average * first_mean)

    def norm(b):
        lanes = slice(b * TOKEN_BLOCK, (b + 1) * TOKEN_BLOCK)
        normed = (hidden[:, lanes] - average[:, lanes]) * inverse[:, lanes]
        rest = scaled[:, lanes] - first_mean[:, lanes] - normed * second_mean[:, lanes]
        HX[b, 0] = (inverse[:, lanes] * rest).astype(BF16)
        FH[:, lanes] = (gain * normed).astype(BF16)

    def hx_first(b):
        return (
            start(copy(HX.at[b, 0], HX.at[b, 3], dev_x(1))),
            start(copy(HX.at[b, 0], HX.at[b, 1], dev_x(NX - 1))),
        )

    def hx_second(b):
        arrived(h1[b])
        return (
            start(copy(HX.at[b, 3, 0:160], HX.at[b, 2, 0:160], dev_x(1))),
            start(copy(HX.at[b, 1, 160:COLS], HX.at[b, 2, 160:COLS], dev_x(NX - 1))),
        )

    h1 = []
    for b in range(NBLOCK):
        norm(b)
        if b < 2:
            h1.append(hx_first(b))
    gradient = jnp.concatenate([HX[b, 0] for b in range(NBLOCK)], axis=1)
    TX[0] = dot(UP[...], gradient).astype(BF16)
    tx = [start(copy(TX.at[0], TX.at[r], dev_x(r))) for r in range(1, NX)]
    UA[...] = ADAPTER_SCALE * dot(inner, gradient, ((1,), (1,)))
    uc = start(copy(UA, UC, other_core))
    HG[...] = gradient
    out_hg = local_copy(HG, hg_out)
    out_fh = local_copy(FH, fh_out)
    h2 = [hx_second(0)]
    h1.append(hx_first(2))
    for c in tx:
        c.wait_recv()
    TZ[0] = jnp.sum(TX[...].astype(F32), axis=0).astype(BF16)
    tz = [start(copy(TZ.at[0], TZ.at[r], dev_z(r))) for r in range(1, NZ)]
    uc.wait_recv()
    UY[0] = UA[...] + UC[...]
    uy = [start(copy(UY.at[0], UY.at[r], dev_y(r))) for r in range(1, NY)]
    h2.append(hx_second(1))
    drain(gathered)
    for c in swaps:
        c.wait_recv()
    exchanged = len(pending)

    halves = NZ * ROWS // 2

    def partials(b):
        arrived(h2[b])

        @pl.loop(0, 2)
        def _(h):
            total = jnp.zeros((halves, TOKEN_BLOCK), F32)
            for r in range(NX):
                w = WX[r, pl.ds(h * (NZ // 2), NZ // 2)].reshape(halves, COLS)
                total = total + dot(w, HX[b, r])
            PART[b, pl.ds(h * (NZ // 2), NZ // 2)] = total.reshape(NZ // 2, ROWS, TOKEN_BLOCK)

    def part(b, rel):
        return PART[b, lax.rem(z + rel, NZ)]

    HALF = ROWS // 2
    rs = {}

    def rs_step(b, step):
        if step == 1:
            for side, three in ((0, 3), (1, 5)):
                lo, hi = (0, HALF) if side == 0 else (HALF, ROWS)
                RS[b, side, 0, 0:HALF] = part(b, 4)[lo:hi].astype(BF16)
                RS[b, side, 1] = part(b, three).astype(BF16)
            rs[b, 1] = (
                start(copy(RS.at[b, 0, 0, 0:HALF], RR.at[b, 0, 0:HALF], dev_z(2))),
                start(copy(RS.at[b, 1, 0, 0:HALF], LR.at[b, 0, 0:HALF], dev_z(NZ - 2))),
                start(copy(RS.at[b, 0, 1], RR.at[b, 1], dev_z(1))),
                start(copy(RS.at[b, 1, 1], LR.at[b, 1], dev_z(NZ - 1))),
            )
            RS[b, 0, 2] = part(b, 1).astype(BF16)
            RS[b, 1, 2] = part(b, 7).astype(BF16)
            rs[b, 4] = (
                start(copy(RS.at[b, 0, 2], RR.at[b, 2], dev_z(1))),
                start(copy(RS.at[b, 1, 2], LR.at[b, 2], dev_z(NZ - 1))),
            )
        else:
            arrived(rs[b, 1])
            right = part(b, 2) + RR[b, 1].astype(F32)
            left = part(b, 6) + LR[b, 1].astype(F32)
            RS[b, 0, 3, 0:HALF] = (right[0:HALF] + RR[b, 0, 0:HALF].astype(F32)).astype(BF16)
            RS[b, 0, 3, HALF:ROWS] = right[HALF:ROWS].astype(BF16)
            RS[b, 1, 3, 0:HALF] = left[0:HALF].astype(BF16)
            RS[b, 1, 3, HALF:ROWS] = (left[HALF:ROWS] + LR[b, 0, 0:HALF].astype(F32)).astype(BF16)
            rs[b, 4] += (
                start(copy(RS.at[b, 0, 3], RR.at[b, 3], dev_z(2))),
                start(copy(RS.at[b, 1, 3], LR.at[b, 3], dev_z(NZ - 2))),
            )

    partials(0)
    rs_step(0, 1)
    h2.append(hx_second(2))
    partials(1)
    rs_step(1, 1)
    for c in tz:
        c.wait_recv()
    through_all = jnp.sum(TZ[...].astype(F32), axis=0).astype(BF16)
    DA[...] = ADAPTER_SCALE * dot(through_all, C[x], ((1,), (1,)))
    dc = start(copy(DA, DC, other_core))
    rs_step(0, 2)
    partials(2)
    rs_step(2, 1)
    dc.wait_recv()
    DY[0] = DA[...] + DC[...]
    dy = [start(copy(DY.at[0], DY.at[r], dev_y(r))) for r in range(1, NY)]
    adapter = ADAPTER_SCALE * dot(DIN[...], through_all, ((0,), (0,)))
    rs_step(1, 2)
    rs_step(2, 2)
    drain(exchanged)
    for c in uy:
        c.wait_recv()
    UG[...] = jnp.sum(UY[...], axis=0)
    out_ug = local_copy(UG, ug_out)
    for c in dy:
        c.wait_recv()
    DG[...] = jnp.sum(DY[...], axis=0)
    out_dg = local_copy(DG, dg_out)
    for b in range(NBLOCK):
        arrived(rs[b, 4])
        lanes = slice(b * TOKEN_BLOCK, (b + 1) * TOKEN_BLOCK)
        total = part(b, 0) + (RR[b, 2].astype(F32) + LR[b, 2].astype(F32))
        total = total + (RR[b, 3].astype(F32) + LR[b, 3].astype(F32))
        CG[:, lanes] = (total + adapter[:, lanes]).astype(BF16)
    out_cg = local_copy(CG, cg_out)

    drain(len(pending))
    for c in (out_hg, out_fh, out_ug, out_dg, out_cg):
        c.wait()


def finish(*refs):
    arrays, outs, held, sems = refs[:5], refs[5:10], refs[10:15], refs[15]
    loads = [pltpu.make_async_copy(a, h, sems.at[0, i]) for i, (a, h) in enumerate(zip(arrays, held))]
    stores = [pltpu.make_async_copy(h, o, sems.at[1, i]) for i, (h, o) in enumerate(zip(held, outs))]
    for c in loads:
        c.start()
    for load, store in zip(loads, stores):
        load.wait()
        store.start()
    for c in stores:
        c.wait()


def on_device(grad, context, residual, gain, codes, exponents, down, up, residue_map, lengths):
    vmem = pl.BlockSpec(memory_space=pltpu.VMEM)
    anywhere = pl.BlockSpec(memory_space=pl.ANY)
    shapes = (
        jax.ShapeDtypeStruct((ROWS, CROP), BF16),
        jax.ShapeDtypeStruct((COLS, CROP), BF16),
        jax.ShapeDtypeStruct((RANK, ROWS), F32),
        jax.ShapeDtypeStruct((RANK, COLS), F32),
        jax.ShapeDtypeStruct((COLS, CROP), BF16),
    )
    results = pl.pallas_call(
        kernel,
        out_shape=shapes,
        in_specs=[anywhere] * 3 + [vmem] + [anywhere] * 5 + [pl.BlockSpec(memory_space=pltpu.SMEM)],
        out_specs=[anywhere] * 5,
        scratch_shapes=[
            pltpu.VMEM((COLS + RANK, DIMS), BF16),
            pltpu.VMEM((NX * NZ, ROWS, CROP), BF16),
            pltpu.VMEM((NX, RANK, 256), BF16),
            pltpu.VMEM((NZ, RANK, NX * ROWS), BF16),
            pltpu.VMEM((COLS, NX * ROWS), BF16),
            pltpu.VMEM((NX, 2, ROWS // 2, COLS), BF16),
            pltpu.VMEM((256, COLS), BF16),
            pltpu.VMEM((NX, NZ, 2, ROWS // 2, COLS), BF16),
            pltpu.VMEM((OWNED, MODEL_WIDTH), BF16),
            pltpu.VMEM((NX, NZ, SLOT, 256), BF16),
            pltpu.VMEM((NX, NZ, SLOT, 256), BF16),
            pltpu.VMEM((NZ, NX, SLOT, 256), BF16),
            pltpu.VMEM((2, 2, NX, SLOT, 256), BF16),
            pltpu.VMEM((NZ // 2, NX, SLOT, 256), BF16),
            pltpu.VMEM((COLS + RANK, CROP), F32),
            pltpu.VMEM((NBLOCK, NX, COLS, TOKEN_BLOCK), BF16),
            pltpu.VMEM((NBLOCK, NZ, ROWS, TOKEN_BLOCK), F32),
            pltpu.VMEM((NBLOCK, 2, 4, ROWS, TOKEN_BLOCK), BF16),
            pltpu.VMEM((NBLOCK, 4, ROWS, TOKEN_BLOCK), BF16),
            pltpu.VMEM((NBLOCK, 4, ROWS, TOKEN_BLOCK), BF16),
            pltpu.VMEM((4, CROP), F32),
            pltpu.VMEM((NX, 4, CROP), F32),
            pltpu.VMEM((NZ, 4, CROP), F32),
            pltpu.VMEM((NX, RANK, CROP), BF16),
            pltpu.VMEM((NZ, RANK, CROP), BF16),
            pltpu.VMEM((RANK, COLS), F32),
            pltpu.VMEM((RANK, COLS), F32),
            pltpu.VMEM((NY, RANK, COLS), F32),
            pltpu.VMEM((RANK, ROWS), F32),
            pltpu.VMEM((RANK, ROWS), F32),
            pltpu.VMEM((NY, RANK, ROWS), F32),
            pltpu.VMEM((COLS, DIMS // BLKR), F32),
            pltpu.VMEM((COLS, CROP), BF16),
            pltpu.VMEM((COLS // BLKC, DIMS // BLKR), jnp.int32),
            pltpu.VMEM((RANK, ROWS), BF16),
            pltpu.VMEM((RANK, COLS), BF16),
            pltpu.VMEM((1, CROP), jnp.int32),
            pltpu.VMEM((ROWS, CROP), BF16),
            pltpu.VMEM((COLS, CROP), BF16),
            pltpu.VMEM((RANK, ROWS), F32),
            pltpu.VMEM((RANK, COLS), F32),
            pltpu.VMEM((COLS, CROP), BF16),
            pltpu.SemaphoreType.DMA((SENDS,)),
            pltpu.SemaphoreType.DMA((SENDS,)),
            pltpu.SemaphoreType.DMA((16,)),
        ],
        compiler_params=pltpu.CompilerParams(
            collective_id=0, has_side_effects=True, vmem_limit_bytes=56 * 1024 * 1024
        ),
        cost_estimate=pl.CostEstimate(flops=2 * 2 * CROP * DIMS * COLS, bytes_accessed=8 << 20, transcendentals=0),
    )(grad, context.T, residual.T, gain, codes.T, exponents.T, down.T, up, residue_map, lengths)
    cg, hg, dg, ug, fh = pl.pallas_call(
        finish,
        out_shape=shapes,
        in_specs=[anywhere] * 5,
        out_specs=[anywhere] * 5,
        scratch_shapes=[pltpu.VMEM(a.shape, a.dtype) for a in shapes] + [pltpu.SemaphoreType.DMA((2, 5))],
    )(*results)
    return cg, hg.T, dg.T, ug, fh.T


def solution(mesh):
    in_specs = (
        P(("dp", "tensor", "section"), None),
        P(("dp", "section"), "tensor"),
        P(("dp", "section"), "tensor"),
        P("tensor"),
        P(None, "tensor"),
        P(None, "tensor"),
        P("tensor", None),
        P(None, "tensor"),
        P(("dp", "section"), None),
        P(("dp", "section")),
    )
    out_specs = (
        P("tensor", ("dp", "section")),
        P(("dp", "section"), "tensor"),
        P("tensor", None),
        P(None, "tensor"),
        P(("dp", "section"), "tensor"),
    )
    return jax.shard_map(
        on_device, mesh=mesh, in_specs=in_specs, out_specs=out_specs, check_vma=False
    )
```
